128 devices in a mesh: seg: 4 (over y), tm: 32 (over z, x, core).
Axes of the slice: x: 4, y: 4, z: 4, core: 2. Of those that a mesh axis runs over, the one named last changes fastest.
Arguments:
- samples: bfloat16 [32, 32768], P('seg', 'tm'), may hold values from -6 to 6
- antenna: bfloat16 [32, 2, 256, 32768], P('seg', None, None, 'tm'), may hold values from -60 to 60
- sky_map: int32 [4096, 32], P(None, 'seg'), may hold values from 0 to 255
- shift_map: int32 [4096, 32], P(None, 'seg'), may hold values from 0 to 7
- owners: int32 [32, 256], P('tm'), may hold values from -1 to 4095, as said below
Outputs:
- fine_stat: float32 [32, 256, 512], P('tm', None, 'seg')
The draws below stay inside these ranges and needn't reach their ends.
Inputs may be any that keep to these rules, and one draw needn't show every extreme that they name: `owners`: every fine template appears exactly once over all lists; each list holds its templates in its first slots and -1 after them; some list is full with 256 templates.
All inputs are finite; a program needn't handle non-finite values.
Results may differ from the reference program's by a relative error of at most 0.0061.
Values may be sent and summed in bfloat16 or wider, within the bound.
A program may use at most 128 MiB of HBM per device.

```python
import math
import jax
import jax.numpy as jnp
from jax import lax

SEGS = 32
SAMPLES = 32768
SKY = 256
BINS = 512
QUARTERS = 8
HALF_WIDTH = 8
TPL_DEV = 128
FINE = 4096
CAP = 256


def draw_antenna(key, part):
    first_key, second_key = jax.random.split(key, 2)
    shape = (SEGS, 2, SKY, SAMPLES)
    ramp = jnp.exp(jnp.linspace(jnp.log(0.5), jnp.log(1.5), SAMPLES)).astype(jnp.float32)
    row_scale = jnp.exp(jax.random.uniform(second_key, (SEGS, 2, SKY, 1), minval=0.0, maxval=jnp.log(10.0)))
    base = jnp.clip(jax.random.normal(first_key, shape), -4.0, 4.0)
    return (base * row_scale * ramp).astype(jnp.bfloat16)


def draw_owners(key, part):
    key_split, key_forced, key_order, key_perm = jax.random.split(key, 4)
    lanes = FINE // TPL_DEV
    pairs = lanes // 2
    split_len = jax.random.randint(key_split, (pairs,), 0, CAP + 1)
    forced = jax.random.randint(key_forced, (), 0, pairs)
    split_len = jnp.where(jnp.arange(pairs) == forced, CAP, split_len)
    lengths = jnp.stack([split_len, CAP - split_len], axis=1).reshape(lanes)
    lengths = lengths[jax.random.permutation(key_order, lanes)]
    offsets = jnp.cumsum(lengths) - lengths
    shuffled = jax.random.permutation(key_perm, FINE)
    slot_pos = jnp.arange(CAP)
    index = jnp.minimum(offsets[:, None] + slot_pos[None, :], FINE - 1)
    return jnp.where(slot_pos[None, :] < lengths[:, None], shuffled[index], -1).astype(jnp.int32)


def set_ends(values, key, least, largest):
    longest = values.shape.index(max(values.shape))
    spots = []
    for shift in (0, 1):
        where = [jax.random.randint(jax.random.fold_in(key, axis), (), 0, length) for axis, length in enumerate(values.shape)]
        where[longest] = (where[longest] + shift) % values.shape[longest]
        spots.append(tuple(where))
    return values.at[spots[0]].set(least).at[spots[1]].set(largest)


def steps_of(rng, extent, cuts, smallest, top_value):
    loudness = 1.0
    for axis_at, parts in cuts:
        steps = jax.random.uniform(jax.random.fold_in(jax.random.fold_in(rng, 6), axis_at), (parts,), jnp.float32, smallest / len(cuts), top_value / len(cuts))
        loudness = loudness * jnp.repeat(jnp.exp(steps), extent[axis_at] // parts).reshape((-1,) + (1,) * (len(extent) - 1 - axis_at))
    return loudness


def noise(own_key, shape, scale, limit, shards=(), kind=jnp.bfloat16):
    level = steps_of(own_key, shape, shards, -0.22, 0.18) if shards else 1.0
    entries = jax.random.normal(own_key, shape, jnp.float32) * scale * level
    return jnp.minimum(jnp.maximum(entries, -limit), limit).astype(kind)


def setup_inputs(seed: int = 0) -> dict:
    keys = jax.random.split(jax.random.key(seed), 6)
    return {
        "samples": noise(keys[0], (SEGS, SAMPLES), 1.0, 6.0, ((0, 4), (1, 32))),
        "antenna": draw_antenna(jax.random.fold_in(keys[5], 71), 0),
        "sky_map": set_ends(jax.random.randint(keys[2], (FINE, SEGS), 0, SKY), jax.random.fold_in(keys[2], 1), 0, SKY - 1).astype(jnp.int32),
        "shift_map": set_ends(jax.random.randint(keys[3], (FINE, SEGS), 0, QUARTERS), jax.random.fold_in(keys[3], 1), 0, QUARTERS - 1).astype(jnp.int32),
        "owners": draw_owners(jax.random.fold_in(keys[5], 71), 0),
    }


epsilon = 1e-6


def dft_table(first_sample, sample_count):
    times = first_sample + jnp.arange(sample_count, dtype=jnp.int32)
    bin_index = jnp.arange(BINS, dtype=jnp.int32)
    phase = (times[:, None] * bin_index[None, :]) % SAMPLES
    angle = phase.astype(jnp.float32) * (2.0 * math.pi / SAMPLES)
    return jnp.concatenate([jnp.cos(angle), jnp.sin(angle)], axis=1).astype(jnp.bfloat16)


def sinc_table():
    source = jnp.arange(BINS).astype(jnp.float32)[:, None, None]
    offsets = (jnp.arange(QUARTERS) - QUARTERS // 2).astype(jnp.float32) * 0.25
    target = jnp.arange(BINS).astype(jnp.float32)[None, None, :]
    spacing = target + offsets[None, :, None] - source
    taper = jnp.where(jnp.abs(spacing) < HALF_WIDTH, jnp.sinc(spacing / HALF_WIDTH), 0.0)
    return (jnp.sinc(spacing) * taper).reshape(BINS, QUARTERS * BINS).astype(jnp.bfloat16)


def statistic(demodulated, square_sums):
    powers = demodulated[..., :BINS] ** 2 + demodulated[..., BINS:] ** 2
    scaled = square_sums / SAMPLES + epsilon
    fstat = jnp.sum(powers / scaled[..., None], axis=-3) / SAMPLES
    return (fstat - jnp.mean(fstat, axis=-1, keepdims=True)).astype(jnp.bfloat16)


def reference(samples, antenna, sky_map, shift_map, owners):
    table = dft_table(0, SAMPLES)

    def segment(inputs):
        series, weights = inputs
        weighted = (weights.astype(jnp.float32) * series.astype(jnp.float32)[None, None, :]).astype(jnp.bfloat16)
        demodulated = jnp.dot(weighted.reshape(2 * SKY, SAMPLES), table, preferred_element_type=jnp.float32)
        demodulated = demodulated.reshape(2, SKY, 2 * BINS)
        wide = weights.astype(jnp.float32)
        square_sums = jnp.sum(wide * wide, axis=2)
        return statistic(demodulated, square_sums)

    coarse = lax.map(segment, (samples, antenna))
    kernel = sinc_table()
    segment_index = jnp.arange(SEGS, dtype=jnp.int32)

    def owner_rows(slot_ids):
        live_slots = slot_ids >= 0
        safe_ids = jnp.maximum(slot_ids, 0)
        sky_sel = sky_map[safe_ids]
        quarter = shift_map[safe_ids]
        coarse_rows = coarse[segment_index[None, :], sky_sel]
        spread = jnp.dot(coarse_rows.reshape(CAP * SEGS, BINS), kernel, preferred_element_type=jnp.float32)
        spread = spread.reshape(CAP, SEGS, QUARTERS, BINS)
        chosen = (quarter[..., None] == jnp.arange(QUARTERS, dtype=jnp.int32)).astype(jnp.float32)
        fine_sum = jnp.sum(jnp.sum(spread * chosen[..., None], axis=2), axis=1)
        return jnp.where(live_slots[:, None], fine_sum, jnp.float32(0.0))

    return lax.map(owner_rows, owners)
```

```python
import math

import jax
import jax.numpy as jnp
import numpy as np
from jax import lax
from jax.sharding import PartitionSpec as P

SAMPLES = 32768
BINS = 512
QUARTERS = 8
HALF_WIDTH = 8
RANK = 60
LANES = 64

epsilon = 1e-06


def time_basis(span):
    half_band = BINS / SAMPLES
    at = np.arange(span, dtype=np.float64)
    diagonal = ((span - 1 - 2 * at) / 2) ** 2 * np.cos(2 * np.pi * half_band)
    beside = at[1:] * (span - at[1:]) / 2
    matrix = np.diag(diagonal) + np.diag(beside, 1) + np.diag(beside, -1)
    vectors = np.linalg.eigh(matrix)[1][:, ::-1][:, :RANK]
    largest = vectors[np.argmax(np.abs(vectors) > 0.02, axis=0), np.arange(RANK)]
    return vectors * np.where(largest < 0, -1.0, 1.0)


def factor_tables(span):
    basis = time_basis(span)
    times = np.arange(SAMPLES).reshape(-1, span)
    bins = np.arange(BINS)
    angle = (times[:, :, None] * bins[None, None, :] % SAMPLES) * (2 * np.pi / SAMPLES)
    table = np.concatenate([np.cos(angle), np.sin(angle)], axis=2)
    expansion = np.einsum("tr,dtk->drk", basis, table, optimize=True)
    return basis, expansion


def sinc_table():
    source = np.arange(BINS)[:, None, None].astype(np.float64)
    offsets = (np.arange(QUARTERS) - QUARTERS // 2) * 0.25
    target = np.arange(BINS)[None, None, :]
    spacing = target + offsets[None, :, None] - source
    taper = np.where(np.abs(spacing) < HALF_WIDTH, np.sinc(spacing / HALF_WIDTH), 0.0)
    return (np.sinc(spacing) * taper).reshape(BINS, QUARTERS * BINS)


def body(samples, antenna, sky_map, shift_map, owners):
    seg_local, span_len = samples.shape
    sky_count = antenna.shape[2]
    basis, expansion = factor_tables(span_len)
    high = basis.astype(jnp.bfloat16)
    low = (basis - high.astype(np.float64)).astype(jnp.bfloat16)
    packed = np.zeros((span_len, 2 * LANES), jnp.bfloat16)
    packed[:, :RANK] = high
    packed[:, LANES : LANES + RANK] = low
    weighted = antenna * samples[:, None, None, :]
    coefs = jnp.dot(
        weighted.reshape(seg_local * 2 * sky_count, span_len),
        jnp.asarray(packed),
        preferred_element_type=jnp.float32,
    )
    coefs = coefs[:, :LANES] + coefs[:, LANES:]
    square_sums = jnp.sum(jnp.square(antenna.astype(jnp.float32)), axis=3).reshape(-1, 1)
    sq_high = square_sums.astype(jnp.bfloat16)
    sq_low = (square_sums - sq_high.astype(jnp.float32)).astype(jnp.bfloat16)
    coefs = jnp.concatenate(
        [coefs[:, :RANK].astype(jnp.bfloat16), sq_high, sq_low, jnp.zeros_like(coefs[:, :2], jnp.bfloat16)], axis=1
    )
    count = expansion.shape[0]
    mine = sky_count // count
    send = coefs.reshape(seg_local, 2, count, mine, LANES).transpose(2, 1, 0, 3, 4).reshape(count, -1, LANES)
    got = lax.all_to_all(send, "tm", 0, 0, tiled=True)
    rows = got.transpose(1, 0, 2).reshape(got.shape[1], -1)
    exp_pad = np.zeros((count, LANES, 2 * BINS), jnp.bfloat16)
    exp_pad[:, :RANK] = expansion
    demodulated = jnp.dot(rows, jnp.asarray(exp_pad).reshape(-1, 2 * BINS), preferred_element_type=jnp.float32)
    sq = jnp.sum(got[:, :, RANK : RANK + 2].astype(jnp.float32), axis=(0, 2))
    powers = demodulated[:, :BINS] ** 2 + demodulated[:, BINS:] ** 2
    scaled = powers / (sq / SAMPLES + epsilon)[:, None]
    fstat = (scaled[: scaled.shape[0] // 2] + scaled[scaled.shape[0] // 2 :]) / SAMPLES
    coarse = (fstat - jnp.mean(fstat, axis=-1, keepdims=True)).astype(jnp.bfloat16)
    coarse = coarse.reshape(seg_local, mine, BINS)
    coarse = lax.all_gather(coarse, "tm", axis=1, tiled=True)

    slot_ids = owners[0]
    live_slots = slot_ids >= 0
    safe_ids = jnp.maximum(slot_ids, 0)
    sky_sel = jnp.transpose(sky_map[safe_ids])
    quarter = jnp.transpose(shift_map[safe_ids])
    onehot = (sky_sel[:, :, None] == jnp.arange(sky_count, dtype=jnp.int32)[None, None, :]).astype(jnp.bfloat16)
    selected = jnp.einsum("scn,snb->scb", onehot, coarse, preferred_element_type=jnp.float32)
    chosen = quarter[..., None] == jnp.arange(QUARTERS, dtype=jnp.int32)
    sums = jnp.sum(jnp.where(chosen[..., None], selected[:, :, None, :], 0.0), axis=0)
    kernel = sinc_table().reshape(BINS, QUARTERS, BINS).transpose(1, 0, 2).reshape(QUARTERS * BINS, BINS)
    fine_sum = jnp.dot(
        sums.astype(jnp.bfloat16).reshape(slot_ids.shape[0], QUARTERS * BINS),
        jnp.asarray(kernel.astype(jnp.bfloat16)),
        preferred_element_type=jnp.float32,
    )
    fine_sum = jnp.where(live_slots[:, None], fine_sum, jnp.float32(0.0))[None]
    return lax.psum_scatter(fine_sum, "seg", scatter_dimension=2, tiled=True)


def solution(mesh):
    in_specs = (
        P("seg", "tm"),
        P("seg", None, None, "tm"),
        P(None, "seg"),
        P(None, "seg"),
        P("tm", None),
    )
    out_specs = P("tm", None, "seg")
    return jax.shard_map(body, mesh=mesh, in_specs=in_specs, out_specs=out_specs, check_vma=False)
```

```python
import functools

import jax
import jax.numpy as jnp
import numpy as np
from jax import lax
from jax.experimental import pallas as pl
from jax.experimental.pallas import tpu as pltpu
from jax.sharding import PartitionSpec as P

SAMPLES = 32768
BINS = 512
QUARTERS = 8
HALF_WIDTH = 8
RANK = 60
LANES = 64
SIDE = 4
MESH = pl.DeviceIdType.MESH

epsilon = 1e-06


def time_basis(span):
    half_band = BINS / SAMPLES
    at = np.arange(span, dtype=np.float64)
    diagonal = ((span - 1 - 2 * at) / 2) ** 2 * np.cos(2 * np.pi * half_band)
    beside = at[1:] * (span - at[1:]) / 2
    matrix = np.diag(diagonal) + np.diag(beside, 1) + np.diag(beside, -1)
    vectors = np.linalg.eigh(matrix)[1][:, ::-1][:, :RANK]
    largest = vectors[np.argmax(np.abs(vectors) > 0.02, axis=0), np.arange(RANK)]
    return vectors * np.where(largest < 0, -1.0, 1.0)


@functools.cache
def factor_tables(span):
    basis = time_basis(span)
    times = np.arange(SAMPLES).reshape(-1, span)
    bins = np.arange(BINS)
    angle = (times[:, :, None] * bins[None, None, :] % SAMPLES) * (2 * np.pi / SAMPLES)
    table = np.concatenate([np.cos(angle), np.sin(angle)], axis=2)
    expansion = np.einsum("tr,dtk->drk", basis, table, optimize=True)
    return basis, expansion


def projection_table(span):
    basis, _ = factor_tables(span)
    high = basis.astype(jnp.bfloat16)
    low = (basis - high.astype(np.float64)).astype(jnp.bfloat16)
    table = np.zeros((2, span, 4, LANES), jnp.bfloat16)
    for a in range(2):
        table[a, :, a, :RANK] = high
        table[a, :, 2 + a, :RANK] = low
    return table.reshape(2 * span, 4 * LANES)


def expansion_table(span):
    _, expansion = factor_tables(span)
    table = np.zeros((expansion.shape[0], LANES, 2 * BINS), jnp.bfloat16)
    table[:, :RANK] = expansion
    return table.reshape(-1, 2 * BINS)


def sinc_table():
    source = np.arange(BINS)[None, :, None].astype(np.float64)
    offsets = ((np.arange(QUARTERS) - QUARTERS // 2) * 0.25)[:, None, None]
    target = np.arange(BINS)[None, None, :]
    spacing = target + offsets - source
    taper = np.where(np.abs(spacing) < HALF_WIDTH, np.sinc(spacing / HALF_WIDTH), 0.0)
    table = (np.sinc(spacing) * taper).astype(jnp.bfloat16)
    return table.reshape(QUARTERS * BINS, 2, BINS // 2).transpose(1, 0, 2)


def kernel(
    samples, owners, sky_map, shift_map, antenna, project_hbm, expand_hbm, sinc_hbm, out,
    ant, project, expand, sinc, weighted, squares, csend, crecv, lhs, cg, onehots, quarters, rows, summed,
    own_part, osend, orecv, in_sem, a_send, a_recv, g_send, g_recv, o_send, o_recv,
):
    seg_local, _, sky_count, span = ant.shape
    peers = crecv.shape[0]
    y = lax.axis_index("seg")
    me = lax.axis_index("tm")
    core = lax.rem(me, 2)
    chip = me // 2
    z = chip // SIDE
    x = lax.rem(chip, SIDE)
    f32, bf16 = jnp.float32, jnp.bfloat16

    loads = [pltpu.make_async_copy(project_hbm, project, in_sem.at[8])]
    loads += [pltpu.make_async_copy(antenna.at[s], ant.at[s], in_sem.at[s]) for s in range(seg_local)]
    loads += [pltpu.make_async_copy(expand_hbm, expand, in_sem.at[9])]
    loads += [pltpu.make_async_copy(sinc_hbm, sinc, in_sem.at[10])]
    for load in loads:
        load.start()

    barrier = pltpu.get_barrier_semaphore()

    def greet(i, carry):
        pl.semaphore_signal(barrier, inc=1, device_id=(y, lax.rem(me + i, peers)), device_id_type=MESH)
        return carry

    lax.fori_loop(1, peers, greet, 0)
    for i in range(1, 4):
        pl.semaphore_signal(barrier, inc=1, device_id=(lax.rem(y + i, 4), me), device_id_type=MESH)

    loads[0].wait()
    series = samples[...].astype(f32)
    chunk = 32
    lane = lax.broadcasted_iota(jnp.int32, (chunk, 128), 1)
    first = (lane == RANK) | (lane == RANK + 1)
    second = (lane == LANES + RANK) | (lane == LANES + RANK + 1)
    wide_lane = lax.broadcasted_iota(jnp.int32, (2 * sky_count, 128), 1)
    low_lane = (wide_lane == RANK + 1) | (wide_lane == LANES + RANK + 1)
    for j in range(seg_local // 2):
        slot = j % 2
        for c in range(2):
            s = 2 * j + c
            loads[1 + s].wait()
            scale = series[s : s + 1].astype(bf16)
            for r in range(0, sky_count, chunk):
                at = c * sky_count + r
                norms = []
                for a in range(2):
                    block = ant[s, a, r : r + chunk, :]
                    weighted[slot, at : at + chunk, a * span : (a + 1) * span] = block * scale
                    block = block.astype(f32)
                    norms.append(jnp.sum(block * block, axis=1, keepdims=True))
                squares[slot, at : at + chunk, :] = jnp.where(first, norms[0], jnp.where(second, norms[1], 0.0))
        coefs = jnp.dot(weighted[slot], project[...], preferred_element_type=f32)
        coefs = coefs[:, :128] + coefs[:, 128:] + squares[slot]
        coefs = jnp.where(low_lane, coefs - coefs.astype(bf16).astype(f32), coefs).astype(bf16)
        for c in range(2):
            csend[c, :, j] = coefs[c * sky_count : (c + 1) * sky_count].reshape(sky_count // 16, 16, 128)

    pl.semaphore_wait(barrier, peers - 1 + 3)

    def coef_copy(i):
        peer = lax.rem(me + i, peers)
        return pltpu.make_async_remote_copy(
            src_ref=csend.at[lax.rem(peer, 2), peer // 2],
            dst_ref=crecv.at[me],
            send_sem=a_send.at[i],
            recv_sem=a_recv.at[me],
            device_id=(y, peer),
            device_id_type=MESH,
        )

    def coef_start(i, carry):
        coef_copy(i).start()
        return carry

    lax.fori_loop(1, peers, coef_start, 0)
    crecv[me] = csend[core, chip]

    ids = owners[...]
    templates = sky_map.shape[1]
    maps = jnp.concatenate(
        [sky_map[...].astype(f32), shift_map[...].astype(f32), jnp.ones((16, templates), f32)], axis=0
    ).astype(bf16)
    slots = ids.shape[1]
    step = 512
    found = jnp.zeros((32, slots), f32)
    for t in range(0, templates, step):
        hit = (lax.broadcasted_iota(jnp.int32, (step, slots), 0) + t == ids).astype(f32).astype(bf16)
        found = found + jnp.dot(maps[:, t : t + step], hit, preferred_element_type=f32)
    diagonal = lax.broadcasted_iota(jnp.int32, (slots, slots), 0) == lax.broadcasted_iota(jnp.int32, (slots, slots), 1)
    found = lax.dot_general(
        diagonal.astype(f32).astype(bf16), found.astype(bf16), (((1,), (1,)), ((), ())), preferred_element_type=f32
    )
    dead = found[:, 16:17] < 0.5
    sky_lane = lax.broadcasted_iota(jnp.int32, (slots, sky_count), 1).astype(f32)
    for s in range(seg_local):
        sky = jnp.where(dead, -1.0, found[:, s : s + 1])
        onehots[s] = jnp.where(sky_lane == sky, 1.0, 0.0).astype(bf16)
        quarters[s] = jnp.broadcast_to(found[:, 8 + s : 9 + s], (slots, 128))

    def coef_wait(i, carry):
        src = lax.rem(me + i, peers)
        pltpu.make_async_remote_copy(
            src_ref=crecv.at[src],
            dst_ref=crecv.at[src],
            send_sem=a_send.at[i],
            recv_sem=a_recv.at[src],
            device_id=(y, src),
            device_id_type=MESH,
        ).wait_recv()
        return carry

    lax.fori_loop(1, peers, coef_wait, 0)
    points = 64
    lane = lax.broadcasted_iota(jnp.int32, (points, 128), 1)
    near = lane < LANES
    sums = [jnp.zeros((points, 128), f32), jnp.zeros((points, 128), f32)]
    for i in range(peers // 2):
        left = crecv[2 * i].reshape(points, 128).astype(f32)
        right = crecv[2 * i + 1].reshape(points, 128).astype(f32)
        turned = pltpu.roll(jnp.where(near, right, left), LANES, 1)
        pair = [jnp.where(near, left, turned), jnp.where(near, turned, right)]
        for a in range(2):
            lhs[a * points : (a + 1) * points, i * 128 : (i + 1) * 128] = pair[a].astype(bf16)
            sums[a] = sums[a] + pair[a]
    loads[1 + seg_local].wait()
    demod = jnp.dot(lhs[...], expand[...], preferred_element_type=f32)
    powers = demod[:, :BINS] * demod[:, :BINS] + demod[:, BINS:] * demod[:, BINS:]
    norm_lane = (lax.rem(lane, LANES) == RANK) | (lax.rem(lane, LANES) == RANK + 1)
    fstat = jnp.zeros((points, BINS), f32)
    for a in range(2):
        norm = jnp.sum(jnp.where(norm_lane, sums[a], 0.0), axis=1, keepdims=True)
        fstat = fstat + powers[a * points : (a + 1) * points] / (norm / SAMPLES + epsilon)
    fstat = fstat / SAMPLES
    coarse = (fstat - jnp.mean(fstat, axis=1, keepdims=True)).astype(bf16)
    cg[chip, core] = coarse.reshape(4, 16, BINS)

    sent = []

    def place(dp, dq):
        zz = lax.rem(z + core * dp + (1 - core) * dq + 2 * SIDE, SIDE)
        xx = lax.rem(x + (1 - core) * dp + core * dq + 2 * SIDE, SIDE)
        return zz * SIDE + xx

    def block_copy(chip_at, core_at, part, device, send_at):
        ref = cg.at[chip_at, core_at]
        if part is not None:
            ref = cg.at[chip_at, core_at, pl.ds(2 * part, 2)]
        return pltpu.make_async_remote_copy(
            src_ref=ref,
            dst_ref=ref,
            send_sem=g_send.at[send_at],
            recv_sem=g_recv.at[(chip_at * 2 + core_at) * 2 + (part or 0)],
            device_id=(y, device),
            device_id_type=MESH,
        )

    def send(block, to, part=None):
        device = chip * 2 + 1 - core if to is None else place(*to) * 2 + core
        copy = block_copy(place(*block), core, part, device, len(sent))
        copy.start()
        sent.append(copy)

    def arrived(block, part=None):
        block_copy(place(*block), core, part, me, 0).wait_recv()

    def spread(block):
        send(block, (0, 1))
        send(block, (0, -1))
        send(block, None)

    send((0, 0), (1, 0))
    send((0, 0), (-1, 0))
    spread((0, 0))
    for side, part in ((-1, 0), (1, 1)):
        arrived((side, 0))
        send((side, 0), (-side, 0), part)
        spread((side, 0))
    for side, part in ((-1, 0), (1, 1)):
        arrived((0, side))
        send((0, side), (0, -side), part)
        send((0, side), None)
    arrived((2, 0), 0)
    arrived((2, 0), 1)
    spread((2, 0))
    for dp in (-1, 1, 2):
        for side, part in ((-1, 0), (1, 1)):
            arrived((dp, side))
            send((dp, side), (0, -side), part)
            send((dp, side), None)
    for dp in (0, -1, 1, 2):
        arrived((dp, 2), 0)
        arrived((dp, 2), 1)
        send((dp, 2), None)

    def other_wait(i, carry):
        block_copy(i, 1 - core, None, me, 0).wait_recv()
        return carry

    lax.fori_loop(0, peers // 2, other_wait, 0)

    for s in range(seg_local):
        picked = cg[:, s % 2, s // 2].reshape(sky_count, BINS)
        rows[s] = jnp.dot(onehots[s], picked, preferred_element_type=f32).astype(bf16)
    chunk = 16

    def group(i, carry):
        at = pl.multiple_of(i * chunk, chunk)
        row = [rows[s, pl.ds(at, chunk), :].astype(f32) for s in range(seg_local)]
        quarter = [quarters[s, pl.ds(at, chunk), :] for s in range(seg_local)]
        quarter = [jnp.concatenate([v] * 4, axis=1) for v in quarter]
        for q in range(QUARTERS):
            total = jnp.zeros((chunk, BINS), f32)
            for s in range(seg_local):
                total = total + jnp.where(quarter[s] == q, row[s], 0.0)
            summed[pl.ds(at, chunk), q * BINS : (q + 1) * BINS] = total.astype(bf16)
        return carry

    lax.fori_loop(0, slots // chunk, group, 0)
    loads[2 + seg_local].wait()

    def part_copy(i, to):
        return pltpu.make_async_remote_copy(
            src_ref=osend.at[to],
            dst_ref=orecv.at[y],
            send_sem=o_send.at[i],
            recv_sem=o_recv.at[y],
            device_id=(to, me),
            device_id_type=MESH,
        )

    half = y // 2
    far = 1 - half
    part = jnp.dot(summed[...], sinc[far], preferred_element_type=f32)
    osend[2 * far] = part[:, :128].astype(bf16)
    osend[2 * far + 1] = part[:, 128:].astype(bf16)
    part_sends = [part_copy(0, 2 * far), part_copy(1, 2 * far + 1)]
    for copy in part_sends:
        copy.start()
    part = jnp.dot(summed[...], sinc[half], preferred_element_type=f32)
    own_part[2 * half] = part[:, :128]
    own_part[2 * half + 1] = part[:, 128:]
    beside = half * 2 + 1 - lax.rem(y, 2)
    osend[beside] = own_part[beside].astype(bf16)
    part_sends.append(part_copy(2, beside))
    part_sends[2].start()
    total = own_part[y]
    for i in range(1, 4):
        src = lax.rem(y + i, 4)
        pltpu.make_async_remote_copy(
            src_ref=orecv.at[src],
            dst_ref=orecv.at[src],
            send_sem=o_send.at[0],
            recv_sem=o_recv.at[src],
            device_id=(src, me),
            device_id_type=MESH,
        ).wait_recv()
        total = total + orecv[src].astype(f32)
    out[...] = total

    def coef_sent(i, carry):
        coef_copy(i).wait_send()
        return carry

    lax.fori_loop(1, peers, coef_sent, 0)
    for copy in sent + part_sends:
        copy.wait_send()


def body(samples, antenna, sky_map, shift_map, owners):
    seg_local, span = samples.shape
    sky_count = antenna.shape[2]
    slots = owners.shape[1]
    peers = SAMPLES // span
    bf16, f32 = jnp.bfloat16, jnp.float32
    vmem = pl.BlockSpec(memory_space=pltpu.VMEM)
    hbm = pl.BlockSpec(memory_space=pl.ANY)
    dma = pltpu.SemaphoreType.DMA
    result = pl.pallas_call(
        kernel,
        out_shape=jax.ShapeDtypeStruct((slots, BINS // 4), f32),
        in_specs=[vmem] * 4 + [hbm] * 4,
        out_specs=vmem,
        scratch_shapes=[
            pltpu.VMEM((seg_local, 2, sky_count, span), bf16),
            pltpu.VMEM((2 * span, 4 * LANES), bf16),
            pltpu.VMEM((peers * LANES, 2 * BINS), bf16),
            pltpu.VMEM((2, QUARTERS * BINS, BINS // 2), bf16),
            pltpu.VMEM((2, 2 * sky_count, 2 * span), bf16),
            pltpu.VMEM((2, 2 * sky_count, 128), f32),
            pltpu.VMEM((2, peers // 2, 4, 16, 128), bf16),
            pltpu.VMEM((peers, 4, 16, 128), bf16),
            pltpu.VMEM((128, peers * LANES), bf16),
            pltpu.VMEM((peers // 2, 2, 4, 16, BINS), bf16),
            pltpu.VMEM((seg_local, slots, sky_count), bf16),
            pltpu.VMEM((seg_local, slots, 128), f32),
            pltpu.VMEM((seg_local, slots, BINS), bf16),
            pltpu.VMEM((slots, QUARTERS * BINS), bf16),
            pltpu.VMEM((4, slots, BINS // 4), f32),
            pltpu.VMEM((4, slots, BINS // 4), bf16),
            pltpu.VMEM((4, slots, BINS // 4), bf16),
            dma((seg_local + 3,)),
            dma((peers,)),
            dma((peers,)),
            dma((40,)),
            dma((2 * peers,)),
            dma((3,)),
            dma((4,)),
        ],
        compiler_params=pltpu.CompilerParams(
            collective_id=0, has_side_effects=True, vmem_limit_bytes=56 * 1024 * 1024
        ),
    )(
        samples,
        owners,
        sky_map.T,
        shift_map.T,
        antenna,
        jnp.asarray(projection_table(span)),
        jnp.asarray(expansion_table(span)),
        jnp.asarray(sinc_table()),
    )
    return result[None]


def solution(mesh):
    in_specs = (
        P("seg", "tm"),
        P("seg", None, None, "tm"),
        P(None, "seg"),
        P(None, "seg"),
        P("tm", None),
    )
    out_specs = P("tm", None, "seg")
    return jax.shard_map(body, mesh=mesh, in_specs=in_specs, out_specs=out_specs, check_vma=False)
```

```python
import functools

import jax
import jax.numpy as jnp
import numpy as np
from jax import lax
from jax.experimental import pallas as pl
from jax.experimental.pallas import tpu as pltpu
from jax.sharding import PartitionSpec as P

SAMPLES = 32768
BINS = 512
QUARTERS = 8
HALF_WIDTH = 8
RANK = 60
LANES = 64
WINDOW = 128
BLOCKS = BINS // WINDOW
SIDE = 4
PARTS = 2
MESH = pl.DeviceIdType.MESH

epsilon = 1e-06


def time_basis(span):
    half_band = BINS / SAMPLES
    at = np.arange(span, dtype=np.float64)
    diagonal = ((span - 1 - 2 * at) / 2) ** 2 * np.cos(2 * np.pi * half_band)
    beside = at[1:] * (span - at[1:]) / 2
    matrix = np.diag(diagonal) + np.diag(beside, 1) + np.diag(beside, -1)
    vectors = np.linalg.eigh(matrix)[1][:, ::-1][:, :RANK]
    largest = vectors[np.argmax(np.abs(vectors) > 0.02, axis=0), np.arange(RANK)]
    return vectors * np.where(largest < 0, -1.0, 1.0)


@functools.cache
def factor_tables(span):
    basis = time_basis(span)
    times = np.arange(SAMPLES).reshape(-1, span)
    bins = np.arange(BINS)
    angle = (times[:, :, None] * bins[None, None, :] % SAMPLES) * (2 * np.pi / SAMPLES)
    table = np.concatenate([np.cos(angle), np.sin(angle)], axis=2)
    expansion = np.einsum("tr,dtk->drk", basis, table, optimize=True)
    return basis, expansion


def projection_table(span):
    basis, _ = factor_tables(span)
    high = basis.astype(jnp.bfloat16)
    low = (basis - high.astype(np.float64)).astype(jnp.bfloat16)
    table = np.zeros((2, span, 4, LANES), jnp.bfloat16)
    for a in range(2):
        table[a, :, a, :RANK] = high
        table[a, :, 2 + a, :RANK] = low
    return table.reshape(2 * span, 4 * LANES)


def expansion_table(span):
    _, expansion = factor_tables(span)
    table = np.zeros((expansion.shape[0], LANES, 2 * BINS), jnp.bfloat16)
    table[:, :RANK] = expansion
    return table.reshape(-1, 2 * BINS)


def edge_owner(lane):
    return (lane + 8) // 16 % 8


def sinc_table():
    edge = np.arange(WINDOW) % 16
    edge = np.where(edge < 8, WINDOW + edge, edge - 16)
    source = np.concatenate([np.arange(WINDOW), edge])[None, :, None].astype(np.float64)
    offsets = ((np.arange(QUARTERS) - QUARTERS // 2) * 0.25)[:, None, None]
    target = np.arange(WINDOW)[None, None, :]
    spacing = target + offsets - source
    taper = np.where(np.abs(spacing) < HALF_WIDTH, np.sinc(spacing / HALF_WIDTH), 0.0)
    return (np.sinc(spacing) * taper).astype(jnp.bfloat16).reshape(QUARTERS * 2 * WINDOW, WINDOW)


def kernel(
    samples, owners, sky_hbm, shift_hbm, antenna, project_hbm, expand_hbm, sinc_hbm, out,
    sky_map, shift_map, ant, project, expand, sinc, weighted, squares, csend, crecv, lhs, cg, onehots, quarters, rows, summed,
    osend, orecv, in_sem, a_send, a_recv, g_send, g_recv, o_send, o_recv,
):
    seg_local, _, sky_count, span = ant.shape
    peers = crecv.shape[1]
    each = crecv.shape[2]
    y = lax.axis_index("seg")
    me = lax.axis_index("tm")
    core = lax.rem(me, 2)
    chip = me // 2
    z = chip // SIDE
    x = lax.rem(chip, SIDE)
    f32, bf16 = jnp.float32, jnp.bfloat16

    load_project = pltpu.make_async_copy(project_hbm, project, in_sem.at[0])
    load_antenna = [pltpu.make_async_copy(antenna.at[s], ant.at[s], in_sem.at[1 + s]) for s in range(seg_local)]
    load_sky = pltpu.make_async_copy(sky_hbm, sky_map, in_sem.at[seg_local + 1])
    load_shift = pltpu.make_async_copy(shift_hbm, shift_map, in_sem.at[seg_local + 2])
    load_expand = pltpu.make_async_copy(expand_hbm, expand, in_sem.at[seg_local + 3])
    load_sinc = pltpu.make_async_copy(sinc_hbm, sinc, in_sem.at[seg_local + 4])
    load_project.start()
    for load in load_antenna:
        load.start()

    barrier = pltpu.get_barrier_semaphore()

    def greet(i, carry):
        pl.semaphore_signal(barrier, inc=1, device_id=(y, lax.rem(me + i, peers)), device_id_type=MESH)
        return carry

    lax.fori_loop(1, peers, greet, 0)
    for i in range(1, 4):
        pl.semaphore_signal(barrier, inc=1, device_id=(lax.rem(y + i, 4), me), device_id_type=MESH)

    load_project.wait()
    series = samples[...].astype(f32)
    chunk = 32
    lane = lax.broadcasted_iota(jnp.int32, (chunk, 128), 1)
    first = (lane == RANK) | (lane == RANK + 1)
    second = (lane == LANES + RANK) | (lane == LANES + RANK + 1)
    wide_lane = lax.broadcasted_iota(jnp.int32, (2 * sky_count, 128), 1)
    low_lane = (wide_lane == RANK + 1) | (wide_lane == LANES + RANK + 1)
    for j in range(seg_local // 2):
        slot = j % 2
        for c in range(2):
            s = 2 * j + c
            load_antenna[s].wait()
            if s == seg_local - 1:
                for load in (load_sky, load_shift, load_expand, load_sinc):
                    load.start()
            scale = series[s : s + 1].astype(bf16)
            for r in range(0, sky_count, chunk):
                at = c * sky_count + r
                norms = []
                for a in range(2):
                    block = ant[s, a, r : r + chunk, :]
                    weighted[slot, at : at + chunk, a * span : (a + 1) * span] = block * scale
                    block = block.astype(f32)
                    norms.append(jnp.sum(block * block, axis=1, keepdims=True))
                squares[slot, at : at + chunk, :] = jnp.where(first, norms[0], jnp.where(second, norms[1], 0.0))
        coefs = jnp.dot(weighted[slot], project[...], preferred_element_type=f32)
        coefs = coefs[:, :128] + coefs[:, 128:] + squares[slot]
        coefs = jnp.where(low_lane, coefs - coefs.astype(bf16).astype(f32), coefs).astype(bf16)
        for c in range(2):
            csend[j // each, c, :, j % each] = coefs[c * sky_count : (c + 1) * sky_count].reshape(sky_count // 16, 16, 128)

    pl.semaphore_wait(barrier, peers - 1 + 3)

    def coef_start(i, part):
        peer = lax.rem(me + 11 * i, peers)
        pltpu.make_async_remote_copy(
            src_ref=csend.at[part, lax.rem(peer, 2), peer // 2],
            dst_ref=crecv.at[part, me],
            send_sem=a_send.at[part],
            recv_sem=a_recv.at[part],
            device_id=(y, peer),
            device_id_type=MESH,
        ).start()
        return part

    for part in range(PARTS):
        lax.fori_loop(1, peers, coef_start, part)
        crecv[part, me] = csend[part, core, chip]

    ids = owners[...]
    load_sky.wait()
    load_shift.wait()
    templates = sky_map.shape[1]
    maps = jnp.concatenate(
        [sky_map[...].astype(f32), shift_map[...].astype(f32), jnp.ones((16, templates), f32)], axis=0
    ).astype(bf16)
    slots = ids.shape[1]
    step = 512
    found = jnp.zeros((32, slots), f32)
    for t in range(0, templates, step):
        hit = (lax.broadcasted_iota(jnp.int32, (step, slots), 0) + t == ids).astype(f32).astype(bf16)
        found = found + jnp.dot(maps[:, t : t + step], hit, preferred_element_type=f32)
    diagonal = lax.broadcasted_iota(jnp.int32, (slots, slots), 0) == lax.broadcasted_iota(jnp.int32, (slots, slots), 1)
    found = lax.dot_general(
        diagonal.astype(f32).astype(bf16), found.astype(bf16), (((1,), (1,)), ((), ())), preferred_element_type=f32
    )
    dead = found[:, 16:17] < 0.5
    sky_lane = lax.broadcasted_iota(jnp.int32, (slots, sky_count), 1).astype(f32)
    for s in range(seg_local):
        sky = jnp.where(dead, -1.0, found[:, s : s + 1])
        onehots[s] = jnp.where(sky_lane == sky, 1.0, 0.0).astype(bf16)
        quarters[s] = jnp.broadcast_to(found[:, 8 + s : 9 + s], (slots, WINDOW))
    owner = edge_owner(lax.broadcasted_iota(jnp.int32, (slots, WINDOW), 1))
    mixed = quarters[0]
    for s in range(1, seg_local):
        mixed = jnp.where(owner == s, quarters[s], mixed)
    quarters[seg_local] = mixed

    def coef_all(part):
        ref = crecv.at[part, pl.ds(0, peers - 1)]
        return pltpu.make_async_remote_copy(
            src_ref=ref,
            dst_ref=ref,
            send_sem=a_send.at[part],
            recv_sem=a_recv.at[part],
            device_id=(y, me),
            device_id_type=MESH,
        )

    def place(dp, dq):
        zz = lax.rem(z + core * dp + (1 - core) * dq, SIDE)
        xx = lax.rem(x + (1 - core) * dp + core * dq, SIDE)
        return zz * SIDE + xx

    def send(part, block, device, sem):
        ref = cg.at[part * peers + place(*block) * 2 + core]
        pltpu.make_async_remote_copy(
            src_ref=ref,
            dst_ref=ref,
            send_sem=g_send,
            recv_sem=g_recv.at[part, sem],
            device_id=(y, device),
            device_id_type=MESH,
        ).start()

    def arrived(part, count, sem):
        ref = cg.at[pl.ds(0, count)]
        pltpu.make_async_remote_copy(
            src_ref=ref,
            dst_ref=ref,
            send_sem=g_send,
            recv_sem=g_recv.at[part, sem],
            device_id=(y, me),
            device_id_type=MESH,
        ).wait_recv()

    sibling = chip * 2 + 1 - core

    def spread(part, dp):
        for dq in range(1, SIDE):
            send(part, (dp, 0), place(0, dq) * 2 + core, SIDE + (SIDE - dp) % SIDE)
        send(part, (dp, 0), sibling, 0)

    points = 16 * each
    lane = lax.broadcasted_iota(jnp.int32, (points, 128), 1)
    near = lane < LANES
    edges = [jnp.zeros((16, WINDOW), f32)] * BLOCKS
    blank = jnp.zeros((points, WINDOW), f32)
    norm_lane = (lax.rem(lane, LANES) == RANK) | (lax.rem(lane, LANES) == RANK + 1)
    for part in range(PARTS):
        coef_all(part).wait_recv()
        sums = [jnp.zeros((points, 128), f32), jnp.zeros((points, 128), f32)]
        for i in range(peers // 2):
            left = crecv[part, 2 * i].reshape(points, 128).astype(f32)
            right = crecv[part, 2 * i + 1].reshape(points, 128).astype(f32)
            turned = pltpu.roll(jnp.where(near, right, left), LANES, 1)
            pair = [jnp.where(near, left, turned), jnp.where(near, turned, right)]
            for a in range(2):
                lhs[part, a * points : (a + 1) * points, i * 128 : (i + 1) * 128] = pair[a].astype(bf16)
                sums[a] = sums[a] + pair[a]
        if part == 0:
            load_expand.wait()
        demod = jnp.dot(lhs[part], expand[...], preferred_element_type=f32)
        powers = demod[:, :BINS] * demod[:, :BINS] + demod[:, BINS:] * demod[:, BINS:]
        fstat = jnp.zeros((points, BINS), f32)
        for a in range(2):
            norm = jnp.sum(jnp.where(norm_lane, sums[a], 0.0), axis=1, keepdims=True)
            fstat = fstat + powers[a * points : (a + 1) * points] / (norm / SAMPLES + epsilon)
        fstat = fstat / SAMPLES
        coarse = (fstat - jnp.mean(fstat, axis=1, keepdims=True)).astype(bf16)
        tiles = [coarse[:, b * WINDOW : (b + 1) * WINDOW] for b in range(BLOCKS)]
        wide = [blank] + [tile.astype(f32) for tile in tiles] + [blank]
        for b in range(BLOCKS):
            turn = lax.rem(b + 2 * BLOCKS - 1 - y, BLOCKS)
            cg[turn * peers + me, part * points : (part + 1) * points, :] = tiles[b]
            edge = jnp.where(lane < 8, wide[b + 2], jnp.where(lane >= WINDOW - 8, wide[b], 0.0))
            for j in range(each):
                shift = 16 * (2 * (part * each + j) + core)
                edges[b] = edges[b] + pltpu.roll(edge[16 * j : 16 * (j + 1)], shift, 1)
            if part == PARTS - 1:
                cg[turn * peers + me, PARTS * points :, :] = edges[b].astype(bf16)
    for turn in range(BLOCKS):
        for dp in range(1, SIDE):
            send(turn, (0, 0), place(dp, 0) * 2 + core, dp)
        spread(turn, 0)

    chunk = 16

    def group(i, carry):
        at = pl.multiple_of(i * chunk, chunk)
        row = [rows[s, pl.ds(at, chunk), :].astype(f32) for s in range(seg_local + 1)]
        quarter = [quarters[s, pl.ds(at, chunk), :] for s in range(seg_local + 1)]
        for q in range(QUARTERS):
            total = jnp.zeros((chunk, WINDOW), f32)
            for s in range(seg_local):
                total = total + jnp.where(quarter[s] == q, row[s], 0.0)
            edge = jnp.where(quarter[seg_local] == q, row[seg_local], 0.0)
            summed[pl.ds(at, chunk), 2 * q * WINDOW : (2 * q + 1) * WINDOW] = total.astype(bf16)
            summed[pl.ds(at, chunk), (2 * q + 1) * WINDOW : (2 * q + 2) * WINDOW] = edge.astype(bf16)
        return carry

    def from_first(turn):
        for dp in range(1, SIDE):
            arrived(turn, 1, SIDE - dp)
            spread(turn, dp)

    def from_second(turn):
        for dp in range(SIDE):
            arrived(turn, SIDE - 1, SIDE + (SIDE - dp) % SIDE)
            for dq in range(1, SIDE):
                send(turn, (dp, dq), sibling, 0)

    def block_sum(turn):
        arrived(turn, peers // 2, 0)
        base = turn * peers
        edge = [cg[base + i, seg_local * 8 :] + cg[base + i + 1, seg_local * 8 :] for i in range(0, peers, 2)]
        edge = jnp.concatenate(edge, axis=0)
        mixed = jnp.zeros((slots, WINDOW), f32)
        for s in range(seg_local):
            at = s // 2 * 16
            main = jnp.concatenate([cg[base + i, at : at + 16] for i in range(s % 2, peers, 2)], axis=0)
            picked = jnp.dot(onehots[s], jnp.concatenate([main, edge], axis=1), preferred_element_type=f32)
            rows[s] = picked[:, :WINDOW].astype(bf16)
            mixed = jnp.where(owner == s, picked[:, WINDOW:], mixed)
        rows[seg_local] = mixed.astype(bf16)
        lax.fori_loop(0, slots // chunk, group, 0)
        if turn == 0:
            load_sinc.wait()
        block = jnp.dot(summed[...], sinc[...], preferred_element_type=f32)
        if turn == BLOCKS - 1:
            return block
        osend[turn] = block.astype(bf16)
        pltpu.make_async_remote_copy(
            src_ref=osend.at[turn],
            dst_ref=orecv.at[y],
            send_sem=o_send,
            recv_sem=o_recv,
            device_id=(lax.rem(y + 1 + turn, BLOCKS), me),
            device_id_type=MESH,
        ).start()

    for turn in range(BLOCKS):
        from_first(turn)
    from_second(0)
    for turn in range(1, BLOCKS):
        from_second(turn)
        block_sum(turn - 1)
    total = block_sum(BLOCKS - 1)
    three = orecv.at[pl.ds(0, BLOCKS - 1)]
    part_all = pltpu.make_async_remote_copy(
        src_ref=three, dst_ref=three, send_sem=o_send, recv_sem=o_recv, device_id=(y, me), device_id_type=MESH
    )
    part_all.wait_recv()
    for i in range(1, BLOCKS):
        total = total + orecv[lax.rem(y + i, BLOCKS)].astype(f32)
    out[...] = total

    for part in range(PARTS):
        coef_all(part).wait_send()
    ref = cg.at[pl.ds(0, BLOCKS * (peers - 1))]
    pltpu.make_async_remote_copy(
        src_ref=ref, dst_ref=ref, send_sem=g_send, recv_sem=g_recv.at[0, 0], device_id=(y, me), device_id_type=MESH
    ).wait_send()
    part_all.wait_send()


def body(samples, antenna, sky_map, shift_map, owners):
    seg_local, span = samples.shape
    sky_count = antenna.shape[2]
    slots = owners.shape[1]
    peers = SAMPLES // span
    each = seg_local // 2 // PARTS
    bf16, f32 = jnp.bfloat16, jnp.float32
    vmem = pl.BlockSpec(memory_space=pltpu.VMEM)
    hbm = pl.BlockSpec(memory_space=pltpu.HBM)
    dma = pltpu.SemaphoreType.DMA
    result = pl.pallas_call(
        kernel,
        out_shape=jax.ShapeDtypeStruct((slots, BINS // 4), f32),
        in_specs=[vmem] * 2 + [hbm] * 6,
        out_specs=vmem,
        scratch_shapes=[
            pltpu.VMEM(sky_map.shape[::-1], jnp.int32),
            pltpu.VMEM(sky_map.shape[::-1], jnp.int32),
            pltpu.VMEM((seg_local, 2, sky_count, span), bf16),
            pltpu.VMEM((2 * span, 4 * LANES), bf16),
            pltpu.VMEM((peers * LANES, 2 * BINS), bf16),
            pltpu.VMEM((QUARTERS * 2 * WINDOW, WINDOW), bf16),
            pltpu.VMEM((2, 2 * sky_count, 2 * span), bf16),
            pltpu.VMEM((2, 2 * sky_count, 128), f32),
            pltpu.VMEM((PARTS, 2, peers // 2, each, 16, 128), bf16),
            pltpu.VMEM((PARTS, peers, each, 16, 128), bf16),
            pltpu.VMEM((PARTS, 32 * each, peers * LANES), bf16),
            pltpu.VMEM((BLOCKS * peers, seg_local * 8 + 16, WINDOW), bf16),
            pltpu.VMEM((seg_local, slots, sky_count), bf16),
            pltpu.VMEM((seg_local + 1, slots, WINDOW), f32),
            pltpu.VMEM((seg_local + 1, slots, WINDOW), bf16),
            pltpu.VMEM((slots, QUARTERS * 2 * WINDOW), bf16),
            pltpu.VMEM((BLOCKS, slots, WINDOW), bf16),
            pltpu.VMEM((BLOCKS, slots, WINDOW), bf16),
            dma((seg_local + 5,)),
            dma((PARTS,)),
            dma((PARTS,)),
            dma,
            dma((BLOCKS, 2 * SIDE)),
            dma,
            dma,
        ],
        compiler_params=pltpu.CompilerParams(
            collective_id=0, has_side_effects=True, vmem_limit_bytes=56 * 1024 * 1024
        ),
    )(
        samples,
        owners,
        sky_map.T,
        shift_map.T,
        antenna,
        jnp.asarray(projection_table(span)),
        jnp.asarray(expansion_table(span)),
        jnp.asarray(sinc_table()),
    )
    return result[None]


def solution(mesh):
    in_specs = (
        P("seg", "tm"),
        P("seg", None, None, "tm"),
        P(None, "seg"),
        P(None, "seg"),
        P("tm", None),
    )
    out_specs = P("tm", None, "seg")
    return jax.shard_map(body, mesh=mesh, in_specs=in_specs, out_specs=out_specs, check_vma=False)
```

```python
import functools

import jax
import jax.numpy as jnp
import numpy as np
from jax import lax
from jax.experimental import pallas as pl
from jax.experimental.pallas import tpu as pltpu
from jax.sharding import PartitionSpec as P

SAMPLES = 32768
BINS = 512
QUARTERS = 8
HALF_WIDTH = 8
RANK = 60
LANES = 64
WINDOW = 128
BLOCKS = BINS // WINDOW
SIDE = 4
PARTS = 2
MESH = pl.DeviceIdType.MESH

epsilon = 1e-06


def time_basis(span):
    half_band = BINS / SAMPLES
    at = np.arange(span, dtype=np.float64)
    diagonal = ((span - 1 - 2 * at) / 2) ** 2 * np.cos(2 * np.pi * half_band)
    beside = at[1:] * (span - at[1:]) / 2
    matrix = np.diag(diagonal) + np.diag(beside, 1) + np.diag(beside, -1)
    vectors = np.linalg.eigh(matrix)[1][:, ::-1][:, :RANK]
    largest = vectors[np.argmax(np.abs(vectors) > 0.02, axis=0), np.arange(RANK)]
    return vectors * np.where(largest < 0, -1.0, 1.0)


@functools.cache
def factor_tables(span):
    basis = time_basis(span)
    times = np.arange(SAMPLES).reshape(-1, span)
    bins = np.arange(BINS)
    angle = (times[:, :, None] * bins[None, None, :] % SAMPLES) * (2 * np.pi / SAMPLES)
    table = np.concatenate([np.cos(angle), np.sin(angle)], axis=2)
    expansion = np.einsum("tr,dtk->drk", basis, table, optimize=True)
    return basis, expansion


def projection_table(span):
    basis, _ = factor_tables(span)
    high = basis.astype(jnp.bfloat16)
    low = (basis - high.astype(np.float64)).astype(jnp.bfloat16)
    table = np.zeros((2, span, 4, LANES), jnp.bfloat16)
    for a in range(2):
        table[a, :, a, :RANK] = high
        table[a, :, 2 + a, :RANK] = low
    return table.reshape(2 * span, 4 * LANES)


def expansion_table(span):
    _, expansion = factor_tables(span)
    table = np.zeros((expansion.shape[0], LANES, 2 * BINS), jnp.bfloat16)
    table[:, :RANK] = expansion
    return table.reshape(-1, 2 * BINS)


def edge_owner(lane):
    return (lane + 8) // 16 % 8


def sinc_table():
    edge = np.arange(WINDOW) % 16
    edge = np.where(edge < 8, WINDOW + edge, edge - 16)
    source = np.concatenate([np.arange(WINDOW), edge])[None, :, None].astype(np.float64)
    offsets = ((np.arange(QUARTERS) - QUARTERS // 2) * 0.25)[:, None, None]
    target = np.arange(WINDOW)[None, None, :]
    spacing = target + offsets - source
    taper = np.where(np.abs(spacing) < HALF_WIDTH, np.sinc(spacing / HALF_WIDTH), 0.0)
    return (np.sinc(spacing) * taper).astype(jnp.bfloat16).reshape(QUARTERS * 2 * WINDOW, WINDOW)


def kernel(
    samples, owners_hbm, sky_hbm, shift_hbm, antenna, project_hbm, expand_hbm, sinc_hbm, out,
    owners, sky_map, shift_map, ant, project, expand, sinc, weighted, squares, csend, crecv, lhs, cg, onehots, quarters, rows, summed,
    osend, orecv, in_sem, a_send, a_recv, g_send, g_recv, o_send, o_recv,
):
    seg_local, _, sky_count, span = ant.shape
    peers = crecv.shape[1]
    each = crecv.shape[2]
    y = lax.axis_index("seg")
    me = lax.axis_index("tm")
    core = lax.rem(me, 2)
    chip = me // 2
    z = chip // SIDE
    x = lax.rem(chip, SIDE)
    f32, bf16 = jnp.float32, jnp.bfloat16

    load_project = pltpu.make_async_copy(project_hbm, project, in_sem.at[0])
    load_antenna = [pltpu.make_async_copy(antenna.at[s], ant.at[s], in_sem.at[1 + s]) for s in range(seg_local)]
    load_owners = pltpu.make_async_copy(owners_hbm, owners, in_sem.at[seg_local + 5])
    load_sky = pltpu.make_async_copy(sky_hbm, sky_map, in_sem.at[seg_local + 1])
    load_shift = pltpu.make_async_copy(shift_hbm, shift_map, in_sem.at[seg_local + 2])
    load_expand = pltpu.make_async_copy(expand_hbm, expand, in_sem.at[seg_local + 3])
    load_sinc = pltpu.make_async_copy(sinc_hbm, sinc, in_sem.at[seg_local + 4])
    load_project.start()
    for load in load_antenna:
        load.start()

    barrier = pltpu.get_barrier_semaphore()

    def greet(i, carry):
        pl.semaphore_signal(barrier, inc=1, device_id=(y, lax.rem(me + i, peers)), device_id_type=MESH)
        return carry

    lax.fori_loop(1, peers, greet, 0)
    for i in range(1, 4):
        pl.semaphore_signal(barrier, inc=1, device_id=(lax.rem(y + i, 4), me), device_id_type=MESH)

    def coef_start(i, part):
        peer = lax.rem(me + 11 * i, peers)
        pltpu.make_async_remote_copy(
            src_ref=csend.at[part, lax.rem(peer, 2), peer // 2],
            dst_ref=crecv.at[part, me],
            send_sem=a_send.at[part],
            recv_sem=a_recv.at[part],
            device_id=(y, peer),
            device_id_type=MESH,
        ).start()
        return part

    load_project.wait()
    series = samples[...].astype(f32)
    chunk = 32
    lane = lax.broadcasted_iota(jnp.int32, (chunk, 128), 1)
    first = (lane == RANK) | (lane == RANK + 1)
    second = (lane == LANES + RANK) | (lane == LANES + RANK + 1)
    wide_lane = lax.broadcasted_iota(jnp.int32, (2 * sky_count, 128), 1)
    low_lane = (wide_lane == RANK + 1) | (wide_lane == LANES + RANK + 1)
    for j in range(seg_local // 2):
        slot = j % 2
        for c in range(2):
            s = 2 * j + c
            load_antenna[s].wait()
            if s == seg_local - 1:
                for load in (load_owners, load_sky, load_shift, load_expand, load_sinc):
                    load.start()
            scale = series[s : s + 1].astype(bf16)
            for r in range(0, sky_count, chunk):
                at = c * sky_count + r
                norms = []
                for a in range(2):
                    block = ant[s, a, r : r + chunk, :]
                    weighted[slot, at : at + chunk, a * span : (a + 1) * span] = block * scale
                    block = block.astype(f32)
                    norms.append(jnp.sum(block * block, axis=1, keepdims=True))
                squares[slot, at : at + chunk, :] = jnp.where(first, norms[0], jnp.where(second, norms[1], 0.0))
        coefs = jnp.dot(weighted[slot], project[...], preferred_element_type=f32)
        coefs = coefs[:, :128] + coefs[:, 128:] + squares[slot]
        coefs = jnp.where(low_lane, coefs - coefs.astype(bf16).astype(f32), coefs).astype(bf16)
        for c in range(2):
            csend[j // each, c, :, j % each] = coefs[c * sky_count : (c + 1) * sky_count].reshape(sky_count // 16, 16, 128)
        if j % each == each - 1:
            if j == each - 1:
                pl.semaphore_wait(barrier, peers - 1 + 3)
            part = j // each
            lax.fori_loop(1, peers, coef_start, part)
            crecv[part, me] = csend[part, core, chip]

    load_owners.wait()
    load_sky.wait()
    load_shift.wait()
    ids = owners[...]
    templates = sky_map.shape[1]
    maps = jnp.concatenate(
        [sky_map[...].astype(f32), shift_map[...].astype(f32), jnp.ones((16, templates), f32)], axis=0
    ).astype(bf16)
    slots = ids.shape[1]
    step = 512
    found = jnp.zeros((32, slots), f32)
    for t in range(0, templates, step):
        hit = (lax.broadcasted_iota(jnp.int32, (step, slots), 0) + t == ids).astype(f32).astype(bf16)
        found = found + jnp.dot(maps[:, t : t + step], hit, preferred_element_type=f32)
    diagonal = lax.broadcasted_iota(jnp.int32, (slots, slots), 0) == lax.broadcasted_iota(jnp.int32, (slots, slots), 1)
    found = lax.dot_general(
        diagonal.astype(f32).astype(bf16), found.astype(bf16), (((1,), (1,)), ((), ())), preferred_element_type=f32
    )
    dead = found[:, 16:17] < 0.5
    sky_lane = lax.broadcasted_iota(jnp.int32, (slots, sky_count), 1).astype(f32)
    for s in range(seg_local):
        sky = jnp.where(dead, -1.0, found[:, s : s + 1])
        onehots[s] = jnp.where(sky_lane == sky, 1.0, 0.0).astype(bf16)
        quarters[s] = jnp.broadcast_to(found[:, 8 + s : 9 + s], (slots, WINDOW))
    owner = edge_owner(lax.broadcasted_iota(jnp.int32, (slots, WINDOW), 1))
    mixed = quarters[0]
    for s in range(1, seg_local):
        mixed = jnp.where(owner == s, quarters[s], mixed)
    quarters[seg_local] = mixed

    def coef_all(part):
        ref = crecv.at[part, pl.ds(0, peers - 1)]
        return pltpu.make_async_remote_copy(
            src_ref=ref,
            dst_ref=ref,
            send_sem=a_send.at[part],
            recv_sem=a_recv.at[part],
            device_id=(y, me),
            device_id_type=MESH,
        )

    def place(dp, dq):
        zz = lax.rem(z + core * dp + (1 - core) * dq, SIDE)
        xx = lax.rem(x + (1 - core) * dp + core * dq, SIDE)
        return zz * SIDE + xx

    def send(part, block, device, sem):
        ref = cg.at[part * peers + place(*block) * 2 + core]
        pltpu.make_async_remote_copy(
            src_ref=ref,
            dst_ref=ref,
            send_sem=g_send,
            recv_sem=g_recv.at[part, sem],
            device_id=(y, device),
            device_id_type=MESH,
        ).start()

    def arrived(part, count, sem):
        ref = cg.at[pl.ds(0, count)]
        pltpu.make_async_remote_copy(
            src_ref=ref,
            dst_ref=ref,
            send_sem=g_send,
            recv_sem=g_recv.at[part, sem],
            device_id=(y, me),
            device_id_type=MESH,
        ).wait_recv()

    sibling = chip * 2 + 1 - core

    def spread(part, dp):
        for dq in range(1, SIDE):
            send(part, (dp, 0), place(0, dq) * 2 + core, SIDE + (SIDE - dp) % SIDE)
        send(part, (dp, 0), sibling, 0)

    points = 16 * each
    lane = lax.broadcasted_iota(jnp.int32, (points, 128), 1)
    near = lane < LANES
    edges = [jnp.zeros((16, WINDOW), f32)] * BLOCKS
    blank = jnp.zeros((points, WINDOW), f32)
    norm_lane = (lax.rem(lane, LANES) == RANK) | (lax.rem(lane, LANES) == RANK + 1)
    for part in range(PARTS):
        coef_all(part).wait_recv()
        sums = [jnp.zeros((points, 128), f32), jnp.zeros((points, 128), f32)]
        for i in range(peers // 2):
            left = crecv[part, 2 * i].reshape(points, 128).astype(f32)
            right = crecv[part, 2 * i + 1].reshape(points, 128).astype(f32)
            turned = pltpu.roll(jnp.where(near, right, left), LANES, 1)
            pair = [jnp.where(near, left, turned), jnp.where(near, turned, right)]
            for a in range(2):
                lhs[part, a * points : (a + 1) * points, i * 128 : (i + 1) * 128] = pair[a].astype(bf16)
                sums[a] = sums[a] + pair[a]
        if part == 0:
            load_expand.wait()
        demod = jnp.dot(lhs[part], expand[...], preferred_element_type=f32)
        powers = demod[:, :BINS] * demod[:, :BINS] + demod[:, BINS:] * demod[:, BINS:]
        fstat = jnp.zeros((points, BINS), f32)
        for a in range(2):
            norm = jnp.sum(jnp.where(norm_lane, sums[a], 0.0), axis=1, keepdims=True)
            fstat = fstat + powers[a * points : (a + 1) * points] / (norm / SAMPLES + epsilon)
        fstat = fstat / SAMPLES
        coarse = (fstat - jnp.mean(fstat, axis=1, keepdims=True)).astype(bf16)
        tiles = [coarse[:, b * WINDOW : (b + 1) * WINDOW] for b in range(BLOCKS)]
        wide = [blank] + [tile.astype(f32) for tile in tiles] + [blank]
        for b in range(BLOCKS):
            turn = lax.rem(b + 2 * BLOCKS - 1 - y, BLOCKS)
            cg[turn * peers + me, part * points : (part + 1) * points, :] = tiles[b]
            edge = jnp.where(lane < 8, wide[b + 2], jnp.where(lane >= WINDOW - 8, wide[b], 0.0))
            for j in range(each):
                shift = 16 * (2 * (part * each + j) + core)
                edges[b] = edges[b] + pltpu.roll(edge[16 * j : 16 * (j + 1)], shift, 1)
            if part == PARTS - 1:
                cg[turn * peers + me, PARTS * points :, :] = edges[b].astype(bf16)
    for turn in range(BLOCKS):
        for dp in range(1, SIDE):
            send(turn, (0, 0), place(dp, 0) * 2 + core, dp)
    for turn in range(BLOCKS):
        spread(turn, 0)

    chunk = 16

    def group(i, carry):
        at = pl.multiple_of(i * chunk, chunk)
        row = [rows[s, pl.ds(at, chunk), :].astype(f32) for s in range(seg_local + 1)]
        quarter = [quarters[s, pl.ds(at, chunk), :] for s in range(seg_local + 1)]
        for q in range(QUARTERS):
            total = jnp.zeros((chunk, WINDOW), f32)
            for s in range(seg_local):
                total = total + jnp.where(quarter[s] == q, row[s], 0.0)
            edge = jnp.where(quarter[seg_local] == q, row[seg_local], 0.0)
            summed[pl.ds(at, chunk), 2 * q * WINDOW : (2 * q + 1) * WINDOW] = total.astype(bf16)
            summed[pl.ds(at, chunk), (2 * q + 1) * WINDOW : (2 * q + 2) * WINDOW] = edge.astype(bf16)
        return carry

    def from_first(turn):
        for dp in range(1, SIDE):
            arrived(turn, 1, SIDE - dp)
            spread(turn, dp)

    def from_second(turn):
        for dp in range(SIDE):
            arrived(turn, SIDE - 1, SIDE + (SIDE - dp) % SIDE)
            for dq in range(1, SIDE):
                send(turn, (dp, dq), sibling, 0)

    def block_sum(turn):
        arrived(turn, peers // 2, 0)
        base = turn * peers
        edge = [cg[base + i, seg_local * 8 :] + cg[base + i + 1, seg_local * 8 :] for i in range(0, peers, 2)]
        edge = jnp.concatenate(edge, axis=0)
        mixed = jnp.zeros((slots, WINDOW), f32)
        for s in range(seg_local):
            at = s // 2 * 16
            main = jnp.concatenate([cg[base + i, at : at + 16] for i in range(s % 2, peers, 2)], axis=0)
            picked = jnp.dot(onehots[s], jnp.concatenate([main, edge], axis=1), preferred_element_type=f32)
            rows[s] = picked[:, :WINDOW].astype(bf16)
            mixed = jnp.where(owner == s, picked[:, WINDOW:], mixed)
        rows[seg_local] = mixed.astype(bf16)
        lax.fori_loop(0, slots // chunk, group, 0)
        if turn == 0:
            load_sinc.wait()
        block = jnp.dot(summed[...], sinc[...], preferred_element_type=f32)
        if turn == BLOCKS - 1:
            return block
        osend[turn] = block.astype(bf16)
        pltpu.make_async_remote_copy(
            src_ref=osend.at[turn],
            dst_ref=orecv.at[y],
            send_sem=o_send,
            recv_sem=o_recv,
            device_id=(lax.rem(y + 1 + turn, BLOCKS), me),
            device_id_type=MESH,
        ).start()

    for turn in range(BLOCKS):
        from_first(turn)
    from_second(0)
    for turn in range(1, BLOCKS):
        from_second(turn)
        block_sum(turn - 1)
    total = block_sum(BLOCKS - 1)
    three = orecv.at[pl.ds(0, BLOCKS - 1)]
    part_all = pltpu.make_async_remote_copy(
        src_ref=three, dst_ref=three, send_sem=o_send, recv_sem=o_recv, device_id=(y, me), device_id_type=MESH
    )
    part_all.wait_recv()
    for i in range(1, BLOCKS):
        total = total + orecv[lax.rem(y + i, BLOCKS)].astype(f32)
    out[...] = total

    for part in range(PARTS):
        coef_all(part).wait_send()
    ref = cg.at[pl.ds(0, BLOCKS * (peers - 1))]
    pltpu.make_async_remote_copy(
        src_ref=ref, dst_ref=ref, send_sem=g_send, recv_sem=g_recv.at[0, 0], device_id=(y, me), device_id_type=MESH
    ).wait_send()
    part_all.wait_send()


def body(samples, antenna, sky_map, shift_map, owners):
    seg_local, span = samples.shape
    sky_count = antenna.shape[2]
    slots = owners.shape[1]
    peers = SAMPLES // span
    each = seg_local // 2 // PARTS
    bf16, f32 = jnp.bfloat16, jnp.float32
    vmem = pl.BlockSpec(memory_space=pltpu.VMEM)
    hbm = pl.BlockSpec(memory_space=pltpu.HBM)
    dma = pltpu.SemaphoreType.DMA
    result = pl.pallas_call(
        kernel,
        out_shape=jax.ShapeDtypeStruct((slots, BINS // 4), f32),
        in_specs=[vmem] + [hbm] * 7,
        out_specs=vmem,
        scratch_shapes=[
            pltpu.VMEM(owners.shape, jnp.int32),
            pltpu.VMEM(sky_map.shape[::-1], jnp.int32),
            pltpu.VMEM(sky_map.shape[::-1], jnp.int32),
            pltpu.VMEM((seg_local, 2, sky_count, span), bf16),
            pltpu.VMEM((2 * span, 4 * LANES), bf16),
            pltpu.VMEM((peers * LANES, 2 * BINS), bf16),
            pltpu.VMEM((QUARTERS * 2 * WINDOW, WINDOW), bf16),
            pltpu.VMEM((2, 2 * sky_count, 2 * span), bf16),
            pltpu.VMEM((2, 2 * sky_count, 128), f32),
            pltpu.VMEM((PARTS, 2, peers // 2, each, 16, 128), bf16),
            pltpu.VMEM((PARTS, peers, each, 16, 128), bf16),
            pltpu.VMEM((PARTS, 32 * each, peers * LANES), bf16),
            pltpu.VMEM((BLOCKS * peers, seg_local * 8 + 16, WINDOW), bf16),
            pltpu.VMEM((seg_local, slots, sky_count), bf16),
            pltpu.VMEM((seg_local + 1, slots, WINDOW), f32),
            pltpu.VMEM((seg_local + 1, slots, WINDOW), bf16),
            pltpu.VMEM((slots, QUARTERS * 2 * WINDOW), bf16),
            pltpu.VMEM((BLOCKS, slots, WINDOW), bf16),
            pltpu.VMEM((BLOCKS, slots, WINDOW), bf16),
            dma((seg_local + 6,)),
            dma((PARTS,)),
            dma((PARTS,)),
            dma,
            dma((BLOCKS, 2 * SIDE)),
            dma,
            dma,
        ],
        compiler_params=pltpu.CompilerParams(
            collective_id=0, has_side_effects=True, vmem_limit_bytes=56 * 1024 * 1024
        ),
    )(
        samples,
        owners,
        sky_map.T,
        shift_map.T,
        antenna,
        jnp.asarray(projection_table(span)),
        jnp.asarray(expansion_table(span)),
        jnp.asarray(sinc_table()),
    )
    return result[None]


def solution(mesh):
    in_specs = (
        P("seg", "tm"),
        P("seg", None, None, "tm"),
        P(None, "seg"),
        P(None, "seg"),
        P("tm", None),
    )
    out_specs = P("tm", None, "seg")
    return jax.shard_map(body, mesh=mesh, in_specs=in_specs, out_specs=out_specs, check_vma=False)
```

```python
import functools

import jax
import jax.numpy as jnp
import numpy as np
from jax import lax
from jax.experimental import pallas as pl
from jax.experimental.pallas import tpu as pltpu
from jax.sharding import PartitionSpec as P

SAMPLES = 32768
BINS = 512
QUARTERS = 8
HALF_WIDTH = 8
RANK = 60
LANES = 64
WINDOW = 128
BLOCKS = BINS // WINDOW
SIDE = 4
PARTS = 2
MESH = pl.DeviceIdType.MESH

epsilon = 1e-06


def time_basis(span):
    half_band = BINS / SAMPLES
    at = np.arange(span, dtype=np.float64)
    diagonal = ((span - 1 - 2 * at) / 2) ** 2 * np.cos(2 * np.pi * half_band)
    beside = at[1:] * (span - at[1:]) / 2
    matrix = np.diag(diagonal) + np.diag(beside, 1) + np.diag(beside, -1)
    vectors = np.linalg.eigh(matrix)[1][:, ::-1][:, :RANK]
    largest = vectors[np.argmax(np.abs(vectors) > 0.02, axis=0), np.arange(RANK)]
    return vectors * np.where(largest < 0, -1.0, 1.0)


@functools.cache
def factor_tables(span):
    basis = time_basis(span)
    times = np.arange(SAMPLES).reshape(-1, span)
    bins = np.arange(BINS)
    angle = (times[:, :, None] * bins[None, None, :] % SAMPLES) * (2 * np.pi / SAMPLES)
    table = np.concatenate([np.cos(angle), np.sin(angle)], axis=2)
    expansion = np.einsum("tr,dtk->drk", basis, table, optimize=True)
    return basis, expansion


def projection_table(span):
    basis, _ = factor_tables(span)
    high = basis.astype(jnp.bfloat16)
    low = (basis - high.astype(np.float64)).astype(jnp.bfloat16)
    table = np.zeros((2, span, 4, LANES), jnp.bfloat16)
    for a in range(2):
        table[a, :, a, :RANK] = high
        table[a, :, 2 + a, :RANK] = low
    return table.reshape(2 * span, 4 * LANES)


def expansion_table(span):
    _, expansion = factor_tables(span)
    table = np.zeros((expansion.shape[0], LANES, 2 * BINS), jnp.bfloat16)
    table[:, :RANK] = expansion
    return table.reshape(-1, 2 * BINS)


def edge_owner(lane):
    return (lane + 8) // 16 % 8


def sinc_table():
    edge = np.arange(WINDOW) % 16
    edge = np.where(edge < 8, WINDOW + edge, edge - 16)
    source = np.concatenate([np.arange(WINDOW), edge])[None, :, None].astype(np.float64)
    offsets = ((np.arange(QUARTERS) - QUARTERS // 2) * 0.25)[:, None, None]
    target = np.arange(WINDOW)[None, None, :]
    spacing = target + offsets - source
    taper = np.where(np.abs(spacing) < HALF_WIDTH, np.sinc(spacing / HALF_WIDTH), 0.0)
    return (np.sinc(spacing) * taper).astype(jnp.bfloat16).reshape(QUARTERS * 2 * WINDOW, WINDOW)


def kernel(
    samples, owners_hbm, sky_hbm, shift_hbm, antenna, project_hbm, expand_hbm, sinc_hbm, out,
    owners, sky_map, shift_map, ant, project, expand, sinc, weighted, squares, csend, crecv, lhs, cg, onehots, quarters, rows, summed,
    osend, orecv, in_sem, a_send, a_recv, g_send, g_recv, o_send, o_recv,
):
    seg_local, _, sky_count, span = ant.shape
    peers = crecv.shape[1]
    each = crecv.shape[2]
    y = lax.axis_index("seg")
    me = lax.axis_index("tm")
    core = lax.rem(me, 2)
    chip = me // 2
    z = chip // SIDE
    x = lax.rem(chip, SIDE)
    f32, bf16 = jnp.float32, jnp.bfloat16

    load_project = pltpu.make_async_copy(project_hbm, project, in_sem.at[0])
    load_antenna = [pltpu.make_async_copy(antenna.at[s], ant.at[s], in_sem.at[1 + s]) for s in range(seg_local)]
    load_owners = pltpu.make_async_copy(owners_hbm, owners, in_sem.at[seg_local + 5])
    load_sky = pltpu.make_async_copy(sky_hbm, sky_map, in_sem.at[seg_local + 1])
    load_shift = pltpu.make_async_copy(shift_hbm, shift_map, in_sem.at[seg_local + 2])
    load_expand = pltpu.make_async_copy(expand_hbm, expand, in_sem.at[seg_local + 3])
    load_sinc = pltpu.make_async_copy(sinc_hbm, sinc, in_sem.at[seg_local + 4])
    load_project.start()
    for load in load_antenna:
        load.start()

    barrier = pltpu.get_barrier_semaphore()

    def greet(i, carry):
        pl.semaphore_signal(barrier, inc=1, device_id=(y, lax.rem(me + i, peers)), device_id_type=MESH)
        return carry

    lax.fori_loop(1, peers, greet, 0)
    for i in range(1, 4):
        pl.semaphore_signal(barrier, inc=1, device_id=(lax.rem(y + i, 4), me), device_id_type=MESH)

    def coef_start(i, part):
        peer = lax.rem(me + 11 * i, peers)
        pltpu.make_async_remote_copy(
            src_ref=csend.at[part, lax.rem(peer, 2), peer // 2],
            dst_ref=crecv.at[part, me],
            send_sem=a_send.at[part],
            recv_sem=a_recv.at[part],
            device_id=(y, peer),
            device_id_type=MESH,
        ).start()
        return part

    load_project.wait()
    series = samples[...].astype(f32)
    chunk = 32
    lane = lax.broadcasted_iota(jnp.int32, (chunk, 128), 1)
    first = (lane == RANK) | (lane == RANK + 1)
    second = (lane == LANES + RANK) | (lane == LANES + RANK + 1)
    wide_lane = lax.broadcasted_iota(jnp.int32, (2 * sky_count, 128), 1)
    low_lane = (wide_lane == RANK + 1) | (wide_lane == LANES + RANK + 1)
    for j in range(seg_local // 2):
        slot = j % 2
        for c in range(2):
            s = 2 * j + c
            load_antenna[s].wait()
            if s == seg_local - 1:
                for load in (load_owners, load_sky, load_shift, load_expand, load_sinc):
                    load.start()
            scale = series[s : s + 1].astype(bf16)
            for r in range(0, sky_count, chunk):
                at = c * sky_count + r
                norms = []
                for a in range(2):
                    block = ant[s, a, r : r + chunk, :]
                    weighted[slot, at : at + chunk, a * span : (a + 1) * span] = block * scale
                    block = block.astype(f32)
                    norms.append(jnp.sum(block * block, axis=1, keepdims=True))
                squares[slot, at : at + chunk, :] = jnp.where(first, norms[0], jnp.where(second, norms[1], 0.0))
        coefs = jnp.dot(weighted[slot], project[...], preferred_element_type=f32)
        coefs = coefs[:, :128] + coefs[:, 128:] + squares[slot]
        coefs = jnp.where(low_lane, coefs - coefs.astype(bf16).astype(f32), coefs).astype(bf16)
        for c in range(2):
            csend[j // each, c, :, j % each] = coefs[c * sky_count : (c + 1) * sky_count].reshape(sky_count // 16, 16, 128)
        if j % each == each - 1:
            if j == each - 1:
                pl.semaphore_wait(barrier, peers - 1 + 3)
            part = j // each
            lax.fori_loop(1, peers, coef_start, part)
            crecv[part, me] = csend[part, core, chip]

    load_owners.wait()
    load_sky.wait()
    load_shift.wait()
    ids = owners[...]
    templates = sky_map.shape[1]
    maps = jnp.concatenate(
        [sky_map[...].astype(f32), shift_map[...].astype(f32), jnp.ones((16, templates), f32)], axis=0
    ).astype(bf16)
    slots = ids.shape[1]
    step = 512
    found = jnp.zeros((32, slots), f32)
    for t in range(0, templates, step):
        hit = (lax.broadcasted_iota(jnp.int32, (step, slots), 0) + t == ids).astype(f32).astype(bf16)
        found = found + jnp.dot(maps[:, t : t + step], hit, preferred_element_type=f32)
    diagonal = lax.broadcasted_iota(jnp.int32, (slots, slots), 0) == lax.broadcasted_iota(jnp.int32, (slots, slots), 1)
    found = lax.dot_general(
        diagonal.astype(f32).astype(bf16), found.astype(bf16), (((1,), (1,)), ((), ())), preferred_element_type=f32
    )
    dead = found[:, 16:17] < 0.5
    sky_lane = lax.broadcasted_iota(jnp.int32, (slots, sky_count), 1).astype(f32)
    for s in range(seg_local):
        sky = jnp.where(dead, -1.0, found[:, s : s + 1])
        onehots[s] = jnp.where(sky_lane == sky, 1.0, 0.0).astype(bf16)
        quarters[s] = jnp.broadcast_to(found[:, 8 + s : 9 + s], (slots, WINDOW))
    owner = edge_owner(lax.broadcasted_iota(jnp.int32, (slots, WINDOW), 1))
    mixed = quarters[0]
    for s in range(1, seg_local):
        mixed = jnp.where(owner == s, quarters[s], mixed)
    quarters[seg_local] = mixed

    def coef_all(part):
        ref = crecv.at[part, pl.ds(0, peers - 1)]
        return pltpu.make_async_remote_copy(
            src_ref=ref,
            dst_ref=ref,
            send_sem=a_send.at[part],
            recv_sem=a_recv.at[part],
            device_id=(y, me),
            device_id_type=MESH,
        )

    def place(dp, dq):
        zz = lax.rem(z + core * dp + (1 - core) * dq, SIDE)
        xx = lax.rem(x + (1 - core) * dp + core * dq, SIDE)
        return zz * SIDE + xx

    def send(part, block, device, sem):
        ref = cg.at[part * peers + place(*block) * 2 + core]
        pltpu.make_async_remote_copy(
            src_ref=ref,
            dst_ref=ref,
            send_sem=g_send,
            recv_sem=g_recv.at[part, sem],
            device_id=(y, device),
            device_id_type=MESH,
        ).start()

    def arrived(part, count, sem):
        ref = cg.at[pl.ds(0, count)]
        pltpu.make_async_remote_copy(
            src_ref=ref,
            dst_ref=ref,
            send_sem=g_send,
            recv_sem=g_recv.at[part, sem],
            device_id=(y, me),
            device_id_type=MESH,
        ).wait_recv()

    sibling = chip * 2 + 1 - core

    def spread(part, dp):
        for dq in range(1, SIDE):
            send(part, (dp, 0), place(0, dq) * 2 + core, SIDE + (SIDE - dp) % SIDE)
        send(part, (dp, 0), sibling, 0)

    points = 16 * each
    lane = lax.broadcasted_iota(jnp.int32, (points, 128), 1)
    near = lane < LANES
    edges = [jnp.zeros((16, WINDOW), f32)] * BLOCKS
    blank = jnp.zeros((points, WINDOW), f32)
    norm_lane = (lax.rem(lane, LANES) == RANK) | (lax.rem(lane, LANES) == RANK + 1)
    for part in range(PARTS):
        coef_all(part).wait_recv()
        sums = [jnp.zeros((points, 128), f32), jnp.zeros((points, 128), f32)]
        for i in range(peers // 2):
            left = crecv[part, 2 * i].reshape(points, 128).astype(f32)
            right = crecv[part, 2 * i + 1].reshape(points, 128).astype(f32)
            turned = pltpu.roll(jnp.where(near, right, left), LANES, 1)
            pair = [jnp.where(near, left, turned), jnp.where(near, turned, right)]
            for a in range(2):
                lhs[part, a * points : (a + 1) * points, i * 128 : (i + 1) * 128] = pair[a].astype(bf16)
                sums[a] = sums[a] + pair[a]
        if part == 0:
            load_expand.wait()
        demod = jnp.dot(lhs[part], expand[...], preferred_element_type=f32)
        powers = demod[:, :BINS] * demod[:, :BINS] + demod[:, BINS:] * demod[:, BINS:]
        fstat = jnp.zeros((points, BINS), f32)
        for a in range(2):
            norm = jnp.sum(jnp.where(norm_lane, sums[a], 0.0), axis=1, keepdims=True)
            fstat = fstat + powers[a * points : (a + 1) * points] / (norm / SAMPLES + epsilon)
        fstat = fstat / SAMPLES
        coarse = (fstat - jnp.mean(fstat, axis=1, keepdims=True)).astype(bf16)
        tiles = [coarse[:, b * WINDOW : (b + 1) * WINDOW] for b in range(BLOCKS)]
        wide = [blank] + [tile.astype(f32) for tile in tiles] + [blank]
        for b in range(BLOCKS):
            turn = lax.rem(b + 2 * BLOCKS - 1 - y, BLOCKS)
            cg[turn * peers + me, part * points : (part + 1) * points, :] = tiles[b]
            edge = jnp.where(lane < 8, wide[b + 2], jnp.where(lane >= WINDOW - 8, wide[b], 0.0))
            for j in range(each):
                shift = 16 * (2 * (part * each + j) + core)
                edges[b] = edges[b] + pltpu.roll(edge[16 * j : 16 * (j + 1)], shift, 1)
            if part == PARTS - 1:
                cg[turn * peers + me, PARTS * points :, :] = edges[b].astype(bf16)
    for turn in range(BLOCKS):
        for dp in range(1, SIDE):
            send(turn, (0, 0), place(dp, 0) * 2 + core, dp)
    for turn in range(BLOCKS):
        spread(turn, 0)

    chunk = 16

    def group(i, carry):
        at = pl.multiple_of(i * chunk, chunk)
        row = [rows[s, pl.ds(at, chunk), :].astype(f32) for s in range(seg_local + 1)]
        quarter = [quarters[s, pl.ds(at, chunk), :] for s in range(seg_local + 1)]
        for q in range(QUARTERS):
            total = jnp.zeros((chunk, WINDOW), f32)
            for s in range(seg_local):
                total = total + jnp.where(quarter[s] == q, row[s], 0.0)
            edge = jnp.where(quarter[seg_local] == q, row[seg_local], 0.0)
            summed[pl.ds(at, chunk), 2 * q * WINDOW : (2 * q + 1) * WINDOW] = total.astype(bf16)
            summed[pl.ds(at, chunk), (2 * q + 1) * WINDOW : (2 * q + 2) * WINDOW] = edge.astype(bf16)
        return carry

    def from_first(turn):
        for dp in range(1, SIDE):
            arrived(turn, 1, SIDE - dp)
            spread(turn, dp)

    def from_second(turn):
        for dp in range(SIDE):
            arrived(turn, SIDE - 1, SIDE + (SIDE - dp) % SIDE)
            for dq in range(1, SIDE):
                send(turn, (dp, dq), sibling, 0)

    def block_sum(turn):
        arrived(turn, peers // 2, 0)
        base = turn * peers
        edge = [cg[base + i, seg_local * 8 :] + cg[base + i + 1, seg_local * 8 :] for i in range(0, peers, 2)]
        edge = jnp.concatenate(edge, axis=0)
        mixed = jnp.zeros((slots, WINDOW), f32)
        for s in range(seg_local):
            at = s // 2 * 16
            main = jnp.concatenate([cg[base + i, at : at + 16] for i in range(s % 2, peers, 2)], axis=0)
            picked = jnp.dot(onehots[s], jnp.concatenate([main, edge], axis=1), preferred_element_type=f32)
            rows[s] = picked[:, :WINDOW].astype(bf16)
            mixed = jnp.where(owner == s, picked[:, WINDOW:], mixed)
        rows[seg_local] = mixed.astype(bf16)
        lax.fori_loop(0, slots // chunk, group, 0, unroll=16)
        if turn == 0:
            load_sinc.wait()
        block = jnp.dot(summed[...], sinc[...], preferred_element_type=f32)
        if turn == BLOCKS - 1:
            return block
        osend[turn] = block.astype(bf16)
        pltpu.make_async_remote_copy(
            src_ref=osend.at[turn],
            dst_ref=orecv.at[y],
            send_sem=o_send,
            recv_sem=o_recv,
            device_id=(lax.rem(y + 1 + turn, BLOCKS), me),
            device_id_type=MESH,
        ).start()

    for turn in range(BLOCKS):
        from_first(turn)
    from_second(0)
    for turn in range(1, BLOCKS):
        from_second(turn)
        block_sum(turn - 1)
    total = block_sum(BLOCKS - 1)
    three = orecv.at[pl.ds(0, BLOCKS - 1)]
    part_all = pltpu.make_async_remote_copy(
        src_ref=three, dst_ref=three, send_sem=o_send, recv_sem=o_recv, device_id=(y, me), device_id_type=MESH
    )
    part_all.wait_recv()
    for i in range(1, BLOCKS):
        total = total + orecv[lax.rem(y + i, BLOCKS)].astype(f32)
    out[...] = total

    for part in range(PARTS):
        coef_all(part).wait_send()
    ref = cg.at[pl.ds(0, BLOCKS * (peers - 1))]
    pltpu.make_async_remote_copy(
        src_ref=ref, dst_ref=ref, send_sem=g_send, recv_sem=g_recv.at[0, 0], device_id=(y, me), device_id_type=MESH
    ).wait_send()
    part_all.wait_send()


def body(samples, antenna, sky_map, shift_map, owners):
    seg_local, span = samples.shape
    sky_count = antenna.shape[2]
    slots = owners.shape[1]
    peers = SAMPLES // span
    each = seg_local // 2 // PARTS
    bf16, f32 = jnp.bfloat16, jnp.float32
    vmem = pl.BlockSpec(memory_space=pltpu.VMEM)
    hbm = pl.BlockSpec(memory_space=pltpu.HBM)
    dma = pltpu.SemaphoreType.DMA
    result = pl.pallas_call(
        kernel,
        out_shape=jax.ShapeDtypeStruct((slots, BINS // 4), f32),
        in_specs=[vmem] + [hbm] * 7,
        out_specs=vmem,
        scratch_shapes=[
            pltpu.VMEM(owners.shape, jnp.int32),
            pltpu.VMEM(sky_map.shape[::-1], jnp.int32),
            pltpu.VMEM(sky_map.shape[::-1], jnp.int32),
            pltpu.VMEM((seg_local, 2, sky_count, span), bf16),
            pltpu.VMEM((2 * span, 4 * LANES), bf16),
            pltpu.VMEM((peers * LANES, 2 * BINS), bf16),
            pltpu.VMEM((QUARTERS * 2 * WINDOW, WINDOW), bf16),
            pltpu.VMEM((2, 2 * sky_count, 2 * span), bf16),
            pltpu.VMEM((2, 2 * sky_count, 128), f32),
            pltpu.VMEM((PARTS, 2, peers // 2, each, 16, 128), bf16),
            pltpu.VMEM((PARTS, peers, each, 16, 128), bf16),
            pltpu.VMEM((PARTS, 32 * each, peers * LANES), bf16),
            pltpu.VMEM((BLOCKS * peers, seg_local * 8 + 16, WINDOW), bf16),
            pltpu.VMEM((seg_local, slots, sky_count), bf16),
            pltpu.VMEM((seg_local + 1, slots, WINDOW), f32),
            pltpu.VMEM((seg_local + 1, slots, WINDOW), bf16),
            pltpu.VMEM((slots, QUARTERS * 2 * WINDOW), bf16),
            pltpu.VMEM((BLOCKS, slots, WINDOW), bf16),
            pltpu.VMEM((BLOCKS, slots, WINDOW), bf16),
            dma((seg_local + 6,)),
            dma((PARTS,)),
            dma((PARTS,)),
            dma,
            dma((BLOCKS, 2 * SIDE)),
            dma,
            dma,
        ],
        compiler_params=pltpu.CompilerParams(
            collective_id=0, has_side_effects=True, vmem_limit_bytes=56 * 1024 * 1024
        ),
    )(
        samples,
        owners,
        sky_map.T,
        shift_map.T,
        antenna,
        jnp.asarray(projection_table(span)),
        jnp.asarray(expansion_table(span)),
        jnp.asarray(sinc_table()),
    )
    return result[None]


def solution(mesh):
    in_specs = (
        P("seg", "tm"),
        P("seg", None, None, "tm"),
        P(None, "seg"),
        P(None, "seg"),
        P("tm", None),
    )
    out_specs = P("tm", None, "seg")
    return jax.shard_map(body, mesh=mesh, in_specs=in_specs, out_specs=out_specs, check_vma=False)
```

```python
import functools

import jax
import jax.numpy as jnp
import numpy as np
from jax import lax
from jax.experimental import pallas as pl
from jax.experimental.pallas import tpu as pltpu
from jax.sharding import PartitionSpec as P

SAMPLES = 32768
BINS = 512
QUARTERS = 8
HALF_WIDTH = 8
RANK = 60
LANES = 64
WINDOW = 128
BLOCKS = BINS // WINDOW
SIDE = 4
PARTS = 2
MESH = pl.DeviceIdType.MESH

epsilon = 1e-06


def time_basis(span):
    half_band = BINS / SAMPLES
    at = np.arange(span, dtype=np.float64)
    diagonal = ((span - 1 - 2 * at) / 2) ** 2 * np.cos(2 * np.pi * half_band)
    beside = at[1:] * (span - at[1:]) / 2
    matrix = np.diag(diagonal) + np.diag(beside, 1) + np.diag(beside, -1)
    vectors = np.linalg.eigh(matrix)[1][:, ::-1][:, :RANK]
    largest = vectors[np.argmax(np.abs(vectors) > 0.02, axis=0), np.arange(RANK)]
    return vectors * np.where(largest < 0, -1.0, 1.0)


@functools.cache
def factor_tables(span):
    basis = time_basis(span)
    times = np.arange(SAMPLES).reshape(-1, span)
    bins = np.arange(BINS)
    angle = (times[:, :, None] * bins[None, None, :] % SAMPLES) * (2 * np.pi / SAMPLES)
    table = np.concatenate([np.cos(angle), np.sin(angle)], axis=2)
    expansion = np.einsum("tr,dtk->drk", basis, table, optimize=True)
    return basis, expansion


def projection_table(span):
    basis, _ = factor_tables(span)
    high = basis.astype(jnp.bfloat16)
    table = np.zeros((span, 2, LANES), jnp.bfloat16)
    table[:, 0, :RANK] = high
    table[:, 1, :RANK] = (basis - high.astype(np.float64)).astype(jnp.bfloat16)
    return table.reshape(span, 2 * LANES)


def expansion_table(span):
    _, expansion = factor_tables(span)
    table = np.zeros((expansion.shape[0], LANES, 2 * BINS), jnp.bfloat16)
    table[:, :RANK] = expansion
    return table.reshape(-1, 2 * BINS)


def edge_owner(lane):
    return (lane + 8) // 16 % 8


def sinc_table():
    edge = np.arange(WINDOW) % 16
    edge = np.where(edge < 8, WINDOW + edge, edge - 16)
    source = np.concatenate([np.arange(WINDOW), edge])[None, :, None].astype(np.float64)
    offsets = ((np.arange(QUARTERS) - QUARTERS // 2) * 0.25)[:, None, None]
    target = np.arange(WINDOW)[None, None, :]
    spacing = target + offsets - source
    taper = np.where(np.abs(spacing) < HALF_WIDTH, np.sinc(spacing / HALF_WIDTH), 0.0)
    return (np.sinc(spacing) * taper).astype(jnp.bfloat16).reshape(QUARTERS * 2 * WINDOW, WINDOW)


def kernel(
    samples, owners_hbm, sky_hbm, shift_hbm, antenna, project_hbm, expand_hbm, sinc_hbm, out,
    owners, sky_map, shift_map, ant, basis, project, expand, sinc, weighted, squares, csend, crecv, lhs, cg, onehots, quarters, rows, summed,
    osend, orecv, in_sem, a_send, a_recv, g_send, g_recv, o_send, o_recv,
):
    seg_local, _, sky_count, span = ant.shape
    peers = crecv.shape[1]
    each = crecv.shape[2]
    y = lax.axis_index("seg")
    me = lax.axis_index("tm")
    core = lax.rem(me, 2)
    chip = me // 2
    z = chip // SIDE
    x = lax.rem(chip, SIDE)
    f32, bf16 = jnp.float32, jnp.bfloat16

    load_project = pltpu.make_async_copy(project_hbm, basis, in_sem.at[0])
    load_antenna = [pltpu.make_async_copy(antenna.at[s], ant.at[s], in_sem.at[1 + s]) for s in range(seg_local)]
    load_owners = pltpu.make_async_copy(owners_hbm, owners, in_sem.at[seg_local + 5])
    load_sky = pltpu.make_async_copy(sky_hbm, sky_map, in_sem.at[seg_local + 1])
    load_shift = pltpu.make_async_copy(shift_hbm, shift_map, in_sem.at[seg_local + 2])
    load_expand = pltpu.make_async_copy(expand_hbm, expand, in_sem.at[seg_local + 3])
    load_sinc = pltpu.make_async_copy(sinc_hbm, sinc, in_sem.at[seg_local + 4])
    load_project.start()
    for load in load_antenna:
        load.start()

    barrier = pltpu.get_barrier_semaphore()

    def greet(i, carry):
        pl.semaphore_signal(barrier, inc=1, device_id=(y, lax.rem(me + i, peers)), device_id_type=MESH)
        return carry

    lax.fori_loop(1, peers, greet, 0)
    for i in range(1, 4):
        pl.semaphore_signal(barrier, inc=1, device_id=(lax.rem(y + i, 4), me), device_id_type=MESH)

    def coef_start(i, part):
        peer = lax.rem(me + 11 * i, peers)
        pltpu.make_async_remote_copy(
            src_ref=csend.at[part, lax.rem(peer, 2), peer // 2],
            dst_ref=crecv.at[part, me],
            send_sem=a_send.at[part],
            recv_sem=a_recv.at[part],
            device_id=(y, peer),
            device_id_type=MESH,
        ).start()
        return part

    load_project.wait()
    straight = basis[...].astype(f32)
    turned = pltpu.roll(straight, LANES, 1)
    front = lax.broadcasted_iota(jnp.int32, straight.shape, 1) < LANES
    project[:span, :128] = jnp.where(front, straight, 0.0).astype(bf16)
    project[:span, 128:] = jnp.where(front, turned, 0.0).astype(bf16)
    project[span:, :128] = jnp.where(front, 0.0, turned).astype(bf16)
    project[span:, 128:] = jnp.where(front, 0.0, straight).astype(bf16)
    series = samples[...].astype(f32)
    chunk = 32
    lane = lax.broadcasted_iota(jnp.int32, (chunk, 128), 1)
    first = (lane == RANK) | (lane == RANK + 1)
    second = (lane == LANES + RANK) | (lane == LANES + RANK + 1)
    wide_lane = lax.broadcasted_iota(jnp.int32, (2 * sky_count, 128), 1)
    low_lane = (wide_lane == RANK + 1) | (wide_lane == LANES + RANK + 1)
    for j in range(seg_local // 2):
        slot = j % 2
        for c in range(2):
            s = 2 * j + c
            load_antenna[s].wait()
            if s == seg_local - 1:
                for load in (load_owners, load_sky, load_shift, load_expand, load_sinc):
                    load.start()
            scale = series[s : s + 1].astype(bf16)
            for r in range(0, sky_count, chunk):
                at = c * sky_count + r
                norms = []
                for a in range(2):
                    block = ant[s, a, r : r + chunk, :]
                    weighted[slot, at : at + chunk, a * span : (a + 1) * span] = block * scale
                    block = block.astype(f32)
                    norms.append(jnp.sum(block * block, axis=1, keepdims=True))
                squares[slot, at : at + chunk, :] = jnp.where(first, norms[0], jnp.where(second, norms[1], 0.0))
        coefs = jnp.dot(weighted[slot], project[...], preferred_element_type=f32)
        coefs = coefs[:, :128] + coefs[:, 128:] + squares[slot]
        coefs = jnp.where(low_lane, coefs - coefs.astype(bf16).astype(f32), coefs).astype(bf16)
        for c in range(2):
            csend[j // each, c, :, j % each] = coefs[c * sky_count : (c + 1) * sky_count].reshape(sky_count // 16, 16, 128)
        if j % each == each - 1:
            if j == each - 1:
                pl.semaphore_wait(barrier, peers - 1 + 3)
            part = j // each
            lax.fori_loop(1, peers, coef_start, part)
            crecv[part, me] = csend[part, core, chip]

    load_owners.wait()
    load_sky.wait()
    load_shift.wait()
    ids = owners[...]
    templates = sky_map.shape[1]
    maps = jnp.concatenate(
        [sky_map[...].astype(f32), shift_map[...].astype(f32), jnp.ones((16, templates), f32)], axis=0
    ).astype(bf16)
    slots = ids.shape[1]
    step = 512
    found = jnp.zeros((32, slots), f32)
    for t in range(0, templates, step):
        hit = (lax.broadcasted_iota(jnp.int32, (step, slots), 0) + t == ids).astype(f32).astype(bf16)
        found = found + jnp.dot(maps[:, t : t + step], hit, preferred_element_type=f32)
    diagonal = lax.broadcasted_iota(jnp.int32, (slots, slots), 0) == lax.broadcasted_iota(jnp.int32, (slots, slots), 1)
    found = lax.dot_general(
        diagonal.astype(f32).astype(bf16), found.astype(bf16), (((1,), (1,)), ((), ())), preferred_element_type=f32
    )
    dead = found[:, 16:17] < 0.5
    sky_lane = lax.broadcasted_iota(jnp.int32, (slots, sky_count), 1).astype(f32)
    for s in range(seg_local):
        sky = jnp.where(dead, -1.0, found[:, s : s + 1])
        onehots[s] = jnp.where(sky_lane == sky, 1.0, 0.0).astype(bf16)
        quarters[s] = jnp.broadcast_to(found[:, 8 + s : 9 + s], (slots, WINDOW))
    owner = edge_owner(lax.broadcasted_iota(jnp.int32, (slots, WINDOW), 1))
    mixed = quarters[0]
    for s in range(1, seg_local):
        mixed = jnp.where(owner == s, quarters[s], mixed)
    quarters[seg_local] = mixed

    def coef_all(part):
        ref = crecv.at[part, pl.ds(0, peers - 1)]
        return pltpu.make_async_remote_copy(
            src_ref=ref,
            dst_ref=ref,
            send_sem=a_send.at[part],
            recv_sem=a_recv.at[part],
            device_id=(y, me),
            device_id_type=MESH,
        )

    def place(dp, dq):
        zz = lax.rem(z + core * dp + (1 - core) * dq, SIDE)
        xx = lax.rem(x + (1 - core) * dp + core * dq, SIDE)
        return zz * SIDE + xx

    def send(part, block, device, sem):
        ref = cg.at[part * peers + place(*block) * 2 + core]
        pltpu.make_async_remote_copy(
            src_ref=ref,
            dst_ref=ref,
            send_sem=g_send,
            recv_sem=g_recv.at[part, sem],
            device_id=(y, device),
            device_id_type=MESH,
        ).start()

    def arrived(part, count, sem):
        ref = cg.at[pl.ds(0, count)]
        pltpu.make_async_remote_copy(
            src_ref=ref,
            dst_ref=ref,
            send_sem=g_send,
            recv_sem=g_recv.at[part, sem],
            device_id=(y, me),
            device_id_type=MESH,
        ).wait_recv()

    sibling = chip * 2 + 1 - core

    def spread(part, dp):
        for dq in range(1, SIDE):
            send(part, (dp, 0), place(0, dq) * 2 + core, SIDE + (SIDE - dp) % SIDE)
        send(part, (dp, 0), sibling, 0)

    points = 16 * each
    lane = lax.broadcasted_iota(jnp.int32, (points, 128), 1)
    near = lane < LANES
    edges = [jnp.zeros((16, WINDOW), f32)] * BLOCKS
    blank = jnp.zeros((points, WINDOW), f32)
    norm_lane = (lax.rem(lane, LANES) == RANK) | (lax.rem(lane, LANES) == RANK + 1)
    for part in range(PARTS):
        coef_all(part).wait_recv()
        sums = [jnp.zeros((points, 128), f32), jnp.zeros((points, 128), f32)]
        for i in range(peers // 2):
            left = crecv[part, 2 * i].reshape(points, 128).astype(f32)
            right = crecv[part, 2 * i + 1].reshape(points, 128).astype(f32)
            turned = pltpu.roll(jnp.where(near, right, left), LANES, 1)
            pair = [jnp.where(near, left, turned), jnp.where(near, turned, right)]
            for a in range(2):
                lhs[part, a * points : (a + 1) * points, i * 128 : (i + 1) * 128] = pair[a].astype(bf16)
                sums[a] = sums[a] + pair[a]
        if part == 0:
            load_expand.wait()
        demod = jnp.dot(lhs[part], expand[...], preferred_element_type=f32)
        powers = demod[:, :BINS] * demod[:, :BINS] + demod[:, BINS:] * demod[:, BINS:]
        fstat = jnp.zeros((points, BINS), f32)
        for a in range(2):
            norm = jnp.sum(jnp.where(norm_lane, sums[a], 0.0), axis=1, keepdims=True)
            fstat = fstat + powers[a * points : (a + 1) * points] / (norm / SAMPLES + epsilon)
        fstat = fstat / SAMPLES
        coarse = (fstat - jnp.mean(fstat, axis=1, keepdims=True)).astype(bf16)
        tiles = [coarse[:, b * WINDOW : (b + 1) * WINDOW] for b in range(BLOCKS)]
        wide = [blank] + [tile.astype(f32) for tile in tiles] + [blank]
        for b in range(BLOCKS):
            turn = lax.rem(b + 2 * BLOCKS - 1 - y, BLOCKS)
            cg[turn * peers + me, part * points : (part + 1) * points, :] = tiles[b]
            edge = jnp.where(lane < 8, wide[b + 2], jnp.where(lane >= WINDOW - 8, wide[b], 0.0))
            for j in range(each):
                shift = 16 * (2 * (part * each + j) + core)
                edges[b] = edges[b] + pltpu.roll(edge[16 * j : 16 * (j + 1)], shift, 1)
            if part == PARTS - 1:
                cg[turn * peers + me, PARTS * points :, :] = edges[b].astype(bf16)
    for turn in range(BLOCKS):
        for dp in range(1, SIDE):
            send(turn, (0, 0), place(dp, 0) * 2 + core, dp)
    for turn in range(BLOCKS):
        spread(turn, 0)

    chunk = 16

    def group(i, carry):
        at = pl.multiple_of(i * chunk, chunk)
        row = [rows[s, pl.ds(at, chunk), :].astype(f32) for s in range(seg_local + 1)]
        quarter = [quarters[s, pl.ds(at, chunk), :] for s in range(seg_local + 1)]
        for q in range(QUARTERS):
            total = jnp.zeros((chunk, WINDOW), f32)
            for s in range(seg_local):
                total = total + jnp.where(quarter[s] == q, row[s], 0.0)
            edge = jnp.where(quarter[seg_local] == q, row[seg_local], 0.0)
            summed[pl.ds(at, chunk), 2 * q * WINDOW : (2 * q + 1) * WINDOW] = total.astype(bf16)
            summed[pl.ds(at, chunk), (2 * q + 1) * WINDOW : (2 * q + 2) * WINDOW] = edge.astype(bf16)
        return carry

    def from_first(turn):
        for dp in range(1, SIDE):
            arrived(turn, 1, SIDE - dp)
            spread(turn, dp)

    def from_second(turn):
        for dp in range(SIDE):
            arrived(turn, SIDE - 1, SIDE + (SIDE - dp) % SIDE)
            for dq in range(1, SIDE):
                send(turn, (dp, dq), sibling, 0)

    def block_sum(turn):
        arrived(turn, peers // 2, 0)
        base = turn * peers
        edge = [cg[base + i, seg_local * 8 :] + cg[base + i + 1, seg_local * 8 :] for i in range(0, peers, 2)]
        edge = jnp.concatenate(edge, axis=0)
        mixed = jnp.zeros((slots, WINDOW), f32)
        for s in range(seg_local):
            at = s // 2 * 16
            main = jnp.concatenate([cg[base + i, at : at + 16] for i in range(s % 2, peers, 2)], axis=0)
            picked = jnp.dot(onehots[s], jnp.concatenate([main, edge], axis=1), preferred_element_type=f32)
            rows[s] = picked[:, :WINDOW].astype(bf16)
            mixed = jnp.where(owner == s, picked[:, WINDOW:], mixed)
        rows[seg_local] = mixed.astype(bf16)
        lax.fori_loop(0, slots // chunk, group, 0, unroll=16)
        if turn == 0:
            load_sinc.wait()
        block = jnp.dot(summed[...], sinc[...], preferred_element_type=f32)
        if turn == BLOCKS - 1:
            return block
        osend[turn] = block.astype(bf16)
        pltpu.make_async_remote_copy(
            src_ref=osend.at[turn],
            dst_ref=orecv.at[y],
            send_sem=o_send,
            recv_sem=o_recv,
            device_id=(lax.rem(y + 1 + turn, BLOCKS), me),
            device_id_type=MESH,
        ).start()

    for turn in range(BLOCKS):
        from_first(turn)
    from_second(0)
    for turn in range(1, BLOCKS):
        from_second(turn)
        block_sum(turn - 1)
    total = block_sum(BLOCKS - 1)
    three = orecv.at[pl.ds(0, BLOCKS - 1)]
    part_all = pltpu.make_async_remote_copy(
        src_ref=three, dst_ref=three, send_sem=o_send, recv_sem=o_recv, device_id=(y, me), device_id_type=MESH
    )
    part_all.wait_recv()
    for i in range(1, BLOCKS):
        total = total + orecv[lax.rem(y + i, BLOCKS)].astype(f32)
    out[...] = total

    for part in range(PARTS):
        coef_all(part).wait_send()
    ref = cg.at[pl.ds(0, BLOCKS * (peers - 1))]
    pltpu.make_async_remote_copy(
        src_ref=ref, dst_ref=ref, send_sem=g_send, recv_sem=g_recv.at[0, 0], device_id=(y, me), device_id_type=MESH
    ).wait_send()
    part_all.wait_send()


def body(samples, antenna, sky_map, shift_map, owners):
    seg_local, span = samples.shape
    sky_count = antenna.shape[2]
    slots = owners.shape[1]
    peers = SAMPLES // span
    each = seg_local // 2 // PARTS
    bf16, f32 = jnp.bfloat16, jnp.float32
    vmem = pl.BlockSpec(memory_space=pltpu.VMEM)
    hbm = pl.BlockSpec(memory_space=pltpu.HBM)
    dma = pltpu.SemaphoreType.DMA
    result = pl.pallas_call(
        kernel,
        out_shape=jax.ShapeDtypeStruct((slots, BINS // 4), f32),
        in_specs=[vmem] + [hbm] * 7,
        out_specs=vmem,
        scratch_shapes=[
            pltpu.VMEM(owners.shape, jnp.int32),
            pltpu.VMEM(sky_map.shape[::-1], jnp.int32),
            pltpu.VMEM(sky_map.shape[::-1], jnp.int32),
            pltpu.VMEM((seg_local, 2, sky_count, span), bf16),
            pltpu.VMEM((span, 2 * LANES), bf16),
            pltpu.VMEM((2 * span, 4 * LANES), bf16),
            pltpu.VMEM((peers * LANES, 2 * BINS), bf16),
            pltpu.VMEM((QUARTERS * 2 * WINDOW, WINDOW), bf16),
            pltpu.VMEM((2, 2 * sky_count, 2 * span), bf16),
            pltpu.VMEM((2, 2 * sky_count, 128), f32),
            pltpu.VMEM((PARTS, 2, peers // 2, each, 16, 128), bf16),
            pltpu.VMEM((PARTS, peers, each, 16, 128), bf16),
            pltpu.VMEM((PARTS, 32 * each, peers * LANES), bf16),
            pltpu.VMEM((BLOCKS * peers, seg_local * 8 + 16, WINDOW), bf16),
            pltpu.VMEM((seg_local, slots, sky_count), bf16),
            pltpu.VMEM((seg_local + 1, slots, WINDOW), f32),
            pltpu.VMEM((seg_local + 1, slots, WINDOW), bf16),
            pltpu.VMEM((slots, QUARTERS * 2 * WINDOW), bf16),
            pltpu.VMEM((BLOCKS, slots, WINDOW), bf16),
            pltpu.VMEM((BLOCKS, slots, WINDOW), bf16),
            dma((seg_local + 6,)),
            dma((PARTS,)),
            dma((PARTS,)),
            dma,
            dma((BLOCKS, 2 * SIDE)),
            dma,
            dma,
        ],
        compiler_params=pltpu.CompilerParams(
            collective_id=0, has_side_effects=True, vmem_limit_bytes=56 * 1024 * 1024
        ),
    )(
        samples,
        owners,
        sky_map.T,
        shift_map.T,
        antenna,
        jnp.asarray(projection_table(span)),
        jnp.asarray(expansion_table(span)),
        jnp.asarray(sinc_table()),
    )
    return result[None]


def solution(mesh):
    in_specs = (
        P("seg", "tm"),
        P("seg", None, None, "tm"),
        P(None, "seg"),
        P(None, "seg"),
        P("tm", None),
    )
    out_specs = P("tm", None, "seg")
    return jax.shard_map(body, mesh=mesh, in_specs=in_specs, out_specs=out_specs, check_vma=False)
```
